1024 devices in a mesh: elem: 128 (over y, z), grp: 8 (over x, core).
Axes of the slice: x: 4, y: 4, z: 32, core: 2. Of those that a mesh axis runs over, the one named last changes fastest.
Arguments:
- prognostic: float32 [2, 32768, 16, 128], P(None, ('elem', 'grp')), may hold values from -6 to 6
- wind_field: float32 [2, 32768, 16, 128], P(None, ('elem', 'grp')), may hold values from -6 to 6
- nbr_slot: int32 [32768, 4], P(('elem', 'grp')), may hold values from 0 to 95
- nbr_edge: int32 [32768, 4], P(('elem', 'grp')), may hold values from 0 to 3
- flip_edge: int32 [32768, 4], P(('elem', 'grp')), may hold values from 0 to 1
- span_dest: int32 [524288, 1], P(('elem', 'grp')), may hold values from 0 to 7; in each aligned block of 512 rows (0 to 511, 512 to 1023, ...) at most 128 rows name the same one
- wet_layers_present: int32 [524288], P(('elem', 'grp')), may hold values from 1 to 128
Outputs:
- dynamics_state: float32 [2, 32768, 16, 128], P(None, ('elem', 'grp'))
- tendency: float32 [2, 32768, 16, 128], P(None, ('elem', 'grp'))
- span_rain: float32 [1024], P(('elem', 'grp'))
- cfl_count: float32 [], replicated
The draws below stay inside these ranges and needn't reach their ends.
Inputs may be any that keep to these rules, and one draw needn't show every extreme that they name: `span_dest`: within the 512 columns of one device at most 128 name the same span, a bound that some block reaches.
All inputs are finite; a program needn't handle non-finite values.
Results may differ from the reference program's by a relative error of at most 0.0003.
Values sent between devices are 32-bit elements; how exact they have to be, the bound alone decides.
A program may use at most 32 MiB of HBM per device.

```python
import math
import jax
import jax.numpy as jnp
import numpy as np
from jax import lax

LEV = 128
NODES = 16
STEPS = 2
E_DEV = 32
ELEMS = 32768
COLS_DEV = 512
COLS = 524288
CAP = 128
N_ELEM = 128
N_GRP = 8


def draw_wind_field(key, part):
    key = jax.random.fold_in(key, 7)
    array_shape = (2, ELEMS, NODES, LEV)
    ramp_scale = 0.3 + 0.9 * jnp.arange(ELEMS, dtype=jnp.float32) / ELEMS
    base_draw = jnp.clip(jax.random.normal(key, array_shape, jnp.float32), -5.0, 5.0)
    return base_draw * ramp_scale[None, :, None, None]


def plant(drawn, stream_key, low, top_value):
    index_at = [jax.random.randint(jax.random.fold_in(stream_key, axis), (), 0, length) for axis, length in enumerate(drawn.shape)]
    widest = drawn.shape.index(max(drawn.shape))
    neighbour = index_at[:widest] + [(index_at[widest] + 1) % drawn.shape[widest]] + index_at[widest + 1:]
    return drawn.at[tuple(index_at)].set(low).at[tuple(neighbour)].set(top_value)


def levels(rng, shape, split, low, high):
    def one(dim, blocks):
        draws = jax.random.uniform(jax.random.fold_in(jax.random.fold_in(rng, 6), dim), (blocks,), jnp.float32, low / len(split), high / len(split))
        return jnp.repeat(jnp.exp(draws), shape[dim] // blocks).reshape((-1,) + (1,) * (len(shape) - dim - 1))

    loudness = one(*split[0])
    for cut in split[1:]:
        loudness = loudness * one(*cut)
    return loudness


def routed_block(own_key, own, number, rows, count, top, limit, slope):
    order = jax.random.permutation(own_key, count)
    crowded, usual = load_shares(count, rows * top, limit, slope, True), load_shares(count, rows * top, limit, slope, False)
    places = jnp.arange(count)

    def named(tallies, rotation):
        used = int((tallies > 0).sum())
        fixed = max(1, used // 4)
        passed = fixed + (places - fixed + rotation * (used - fixed)) % max(1, count - fixed)
        return jnp.zeros((count,), jnp.int32).at[order[jnp.where(places < fixed, places, passed)]].set(jnp.asarray(tallies, jnp.int32))

    tallies = jnp.where(number % 4 == 0, named(crowded, number // 4), named(usual, number - number // 4 - 1))
    mixed = jax.random.permutation(jax.random.fold_in(own, 3), count)
    donor, receiver = mixed[0:count // 2 * 2:2], mixed[1:count // 2 * 2:2]
    slack = jnp.minimum(tallies[donor] - 1, limit - tallies[receiver]) // 2
    slack = jnp.where((donor == order[0]) | (receiver == order[0]) | (tallies[receiver] == 0), 0, jnp.maximum(slack, 0))
    passed = jax.random.randint(jax.random.fold_in(own, 4), (count // 2,), 0, 1 << 20) % (slack + 1)
    tallies = tallies.at[donor].add(-passed).at[receiver].add(passed)
    items = jnp.searchsorted(jnp.cumsum(tallies), jnp.arange(rows * top), side="right").astype(jnp.int32)
    listing = items.reshape(top, rows).T
    listing = listing[jax.random.permutation(jax.random.fold_in(own, 1), rows)]
    rotation = jax.random.randint(jax.random.fold_in(own, 2), (rows, 1), 0, top)
    return jnp.take_along_axis(listing, (jnp.arange(top)[None, :] + rotation) % top, axis=1)


def load_shares(count, total, limit, slope, full):
    weights = [(1 << 20) // math.isqrt(standing ** slope) + 1 for standing in range(1, count + 1)]
    largest = limit if full else min(limit, max(-(-total // count), total * weights[0] // sum(weights)))
    least = 1 if total - largest >= count - 1 else 0
    holding, surplus = [largest] + [least] * (count - 1), total - largest - least * (count - 1)
    while surplus > 0:
        candidates = [i for i in range(1, count) if holding[i] < largest] or [i for i in range(1, count) if holding[i] < limit]
        pool, budget = sum([weights[i] for i in candidates]), surplus
        for i in candidates:
            addition = min(limit - holding[i], max(1, budget * weights[i] // pool), surplus)
            holding[i] = holding[i] + addition
            surplus = surplus - addition
    return np.array(holding)


def centred(own_key, dims, spread, reach, cuts=(), kind=jnp.bfloat16):
    gain = levels(own_key, dims, cuts, -0.22, 0.18) if cuts else 1.0
    entries = jax.random.normal(own_key, dims, jnp.float32) * spread * gain
    return jnp.minimum(jnp.maximum(entries, -reach), reach).astype(kind)


def setup_inputs(seed: int = 0) -> dict:
    keys = jax.random.split(jax.random.key(seed), 8)
    prognostic = centred(keys[0], (2, ELEMS, NODES, LEV), 1.0, 6.0, ((1, 1024),), jnp.float32)
    wind_field = draw_wind_field(jax.random.fold_in(keys[7], 71), 0)
    nbr_slot = plant(jax.random.randint(keys[2], (ELEMS, 4), 0, 3 * E_DEV), jax.random.fold_in(keys[2], 1), 0, (3 * E_DEV) - 1).astype(jnp.int32)
    nbr_edge = plant(jax.random.randint(keys[3], (ELEMS, 4), 0, 4), jax.random.fold_in(keys[3], 1), 0, 3).astype(jnp.int32)
    flip_edge = plant(jax.random.randint(keys[4], (ELEMS, 4), 0, 2), jax.random.fold_in(keys[4], 1), 0, 1).astype(jnp.int32)
    span_dest_keys = jax.random.split(jax.random.fold_in(keys[5], 1), COLS // COLS_DEV)
    span_dest_turns = jax.random.permutation(jax.random.fold_in(keys[5], 3), COLS // COLS_DEV)
    span_dest = jax.vmap(lambda own, number: routed_block(jax.random.fold_in(keys[5], 2), own, number, COLS_DEV, N_GRP, 1, CAP, 2))(span_dest_keys, span_dest_turns).reshape((COLS, 1))
    wet_layers_present = plant(jax.random.randint(keys[6], (COLS,), 1, LEV + 1), jax.random.fold_in(keys[6], 1), 1, LEV).astype(jnp.int32)
    return dict(prognostic=prognostic, wind_field=wind_field, nbr_slot=nbr_slot, nbr_edge=nbr_edge, flip_edge=flip_edge, span_dest=span_dest, wet_layers_present=wet_layers_present)


edge_nodes = np.array([[0, 1, 2, 3], [3, 7, 11, 15], [12, 13, 14, 15], [0, 4, 8, 12]])
time_step = 0.02
viscosity = 0.05
penalty = 4.0
cfl_limit = 2.0
latent = 1.5
evap_rate = 0.02

def nodal_derivative_matrix():
    points = np.array([-1.0, -1.0 / math.sqrt(5.0), 1.0 / math.sqrt(5.0), 1.0])
    off_diag = points[:, None] - points[None, :] + np.eye(4)
    weights = 1.0 / np.prod(off_diag, axis=1)
    derivative = weights[None, :] / weights[:, None] / off_diag
    derivative = derivative * (1.0 - np.eye(4))
    return derivative - np.eye(4) * np.sum(derivative, axis=1)[:, None]

def advance(fields, wind_field, jump_term):
    elements = fields.shape[1]
    layer_total = fields.shape[-1]
    shaped = fields.reshape(2, elements, 4, 4, layer_total)
    derivative = jnp.asarray(nodal_derivative_matrix(), jnp.float32)
    second = jnp.asarray(nodal_derivative_matrix() @ nodal_derivative_matrix(), jnp.float32)
    highest = lax.Precision.HIGHEST
    grad_col = jnp.einsum('ab,zerbl->zeral', derivative, shaped, precision=highest)
    grad_row = jnp.einsum('ab,zebcl->zeacl', derivative, shaped, precision=highest)
    laplace = jnp.einsum('ab,zerbl->zeral', second, shaped, precision=highest)
    laplace = laplace + jnp.einsum('ab,zebcl->zeacl', second, shaped, precision=highest)
    grad_col = grad_col.reshape(fields.shape)
    grad_row = grad_row.reshape(fields.shape)
    laplace = laplace.reshape(fields.shape)
    rate = -(wind_field[0][None] * grad_col + wind_field[1][None] * grad_row) + viscosity * laplace
    for edge_side in range(4):
        rate = rate.at[:, :, edge_nodes[edge_side], :].add(penalty * jump_term[:, :, edge_side])
    return fields + time_step * rate

def vertical_profile_update(thermal_state_kelvin, humidity_mixing_ratio, wet_layers_present):
    layer_total = thermal_state_kelvin.shape[-1]
    heights = jnp.arange(layer_total)
    level_mask = (heights < wet_layers_present[..., None]).astype(jnp.float32)
    condensing_threshold = 0.5 * jnp.exp(0.3 * thermal_state_kelvin)
    condense = 0.5 * jax.nn.softplus(2.0 * (humidity_mixing_ratio - condensing_threshold)) * level_mask
    above_mask = (heights[:, None] > heights[None, :]).astype(jnp.float32)
    rain_flux = jnp.matmul(condense, above_mask, precision=lax.Precision.HIGHEST)
    evaporate = evap_rate * rain_flux * level_mask
    warming_source = latent * (condense - evaporate)
    drying = evaporate - condense
    column_rain = lax.optimization_barrier(jnp.sum(condense - evaporate, axis=-1))
    return (warming_source, drying, column_rain)

def reference(prognostic, wind_field, nbr_slot, nbr_edge, flip_edge, span_dest, wet_layers_present):
    elements = prognostic.shape[1]
    element_ids = jnp.arange(elements)
    block_ids = element_ids // E_DEV
    position = block_ids // N_GRP
    group_ids = block_ids % N_GRP
    offset = nbr_slot // E_DEV - 1
    nbr_block = (position[:, None] + offset) % N_ELEM * N_GRP + group_ids[:, None]
    neighbours = nbr_block * E_DEV + nbr_slot % E_DEV
    fields = prognostic
    for dyn_step in range(STEPS):
        traces = fields[:, :, edge_nodes, :]
        across = traces[:, neighbours, nbr_edge]
        across = jnp.where(flip_edge[None, :, :, None, None] == 1, across[..., ::-1, :], across)
        fields = advance(fields, wind_field, across - traces)
    warming_source, drying, column_rain = vertical_profile_update(fields[0], fields[1], wet_layers_present.reshape(elements, 16))
    tendency = jnp.stack([warming_source, drying])
    owners = jnp.arange(elements * 16) // COLS_DEV // N_GRP * N_GRP + span_dest[:, 0]
    span_rain = jax.ops.segment_sum(column_rain.reshape(-1), owners, num_segments=N_ELEM * N_GRP) / COLS_DEV
    lowest_level = jnp.abs(wind_field[0, :, :, 0]) + jnp.abs(wind_field[1, :, :, 0])
    cfl_count = jnp.sum((lowest_level > cfl_limit).astype(jnp.float32))
    return (fields, tendency, span_rain, cfl_count)
```

```python
import math

import jax
import jax.numpy as jnp
import numpy as np
from jax import lax
from jax.experimental import pallas as pl
from jax.experimental.pallas import tpu as pltpu
from jax.sharding import PartitionSpec as P

STEPS = 2
ELEMS = 32
ROWS = 512
LEV = 128
EDGE_ROWS = 384

edge_nodes = np.array([[0, 1, 2, 3], [3, 7, 11, 15], [12, 13, 14, 15], [0, 4, 8, 12]])
time_step = 0.02
viscosity = 0.05
penalty = 4.0
cfl_limit = 2.0
latent = 1.5
evap_rate = 0.02

ORDER = [0, 1, 2, 3, 4, 7, 8, 11, 12, 13, 14, 15, 5, 6, 9, 10]
PLACE = {n: p for p, n in enumerate(ORDER)}
EDGE_PLACE = [[PLACE[int(n)] for n in nodes] for nodes in edge_nodes]
SIDES = {n: [(s, i) for s in range(4) for i in range(4) if edge_nodes[s][i] == n] for n in range(16)}

Z_CHIPS = 32
MESH = pl.DeviceIdType.MESH


def nodal_derivative_matrix():
    points = np.array([-1.0, -1.0 / math.sqrt(5.0), 1.0 / math.sqrt(5.0), 1.0])
    off_diag = points[:, None] - points[None, :] + np.eye(4)
    weights = 1.0 / np.prod(off_diag, axis=1)
    derivative = weights[None, :] / weights[:, None] / off_diag
    derivative = derivative * (1.0 - np.eye(4))
    return derivative - np.eye(4) * np.sum(derivative, axis=1)[:, None]


D1 = nodal_derivative_matrix()
D2 = D1 @ D1


def weighted(coefs, values):
    total = None
    for coef, value in zip(coefs, values):
        if abs(coef) < 1e-12:
            continue
        term = value * np.float32(coef)
        total = term if total is None else total + term
    return total


def split_rows(src, dst, rows):
    step = 64

    def body(k, carry):
        at = pl.ds(pl.multiple_of(k * step, step), step)
        x = src[at, :]
        high = x.astype(jnp.bfloat16)
        dst[at, 0:LEV] = high
        dst[at, LEV : 2 * LEV] = (x - high.astype(jnp.float32)).astype(jnp.bfloat16)
        return carry

    lax.fori_loop(0, rows // step, body, 0)


def local_step(src, wind, base, f):
    def body(k, carry):
        at = lambda n: pl.ds(pl.multiple_of(PLACE[n] * ELEMS + k * 8, 8), 8)
        F = [src[f, at(n), :] for n in range(16)]
        for n in range(16):
            r, c = divmod(n, 4)
            row = [F[4 * r + b] for b in range(4)]
            col = [F[4 * b + c] for b in range(4)]
            u = wind[0, pl.ds(k * 128 + n, 8, stride=16), :]
            v = wind[1, pl.ds(k * 128 + n, 8, stride=16), :]
            grad_col = weighted(D1[c] * -time_step, row)
            grad_row = weighted(D1[r] * -time_step, col)
            centre = 1.0 - time_step * penalty * len(SIDES[n])
            centre = centre + time_step * viscosity * (D2[c][c] + D2[r][r])
            others = [b for b in range(4) if b != c]
            others_r = [b for b in range(4) if b != r]
            lap = weighted(
                [centre]
                + [time_step * viscosity * D2[c][b] for b in others]
                + [time_step * viscosity * D2[r][b] for b in others_r],
                [F[n]] + [row[b] for b in others] + [col[b] for b in others_r],
            )
            base[f, at(n), :] = lap + u * grad_col + v * grad_row
        return carry

    lax.fori_loop(0, ELEMS // 8, body, 0)


def sum_rows(x):
    return jnp.sum(x, axis=0, keepdims=True)


def kernel(
    prog, wind, slot, edge, flip, dest, wet,
    dyn, tend, rain, cfl,
    praw, wraw, islot, iedge, iflip, idest, iwet,
    p0, p1, base, recv, jm, rhs, rhs_own, tq, bt, cols, cond, condf, obuf, tbuf,
    cval, crecv, part, precv,
    in_sem, hs_sem, hr_sem, cs_sem, cr_sem, rs_sem, rr_sem, out_sem,
):
    f32, bf16 = jnp.float32, jnp.bfloat16
    me = lax.axis_index("elem")
    grp = lax.axis_index("grp")
    n_elem = lax.axis_size("elem")
    nxt, prv = lax.rem(me + 1, n_elem), lax.rem(me + n_elem - 1, n_elem)
    y, z = me // Z_CHIPS, lax.rem(me, Z_CHIPS)
    zh, zl = z // 4, lax.rem(z, 4)
    grp_peers = [(me, lax.rem(grp + k, 8)) for k in range(1, 8)]
    y_peers = [(lax.rem(y + k, 4) * Z_CHIPS + z, grp) for k in range(1, 4)]
    zl_peers = [(y * Z_CHIPS + zh * 4 + lax.rem(zl + k, 4), grp) for k in range(1, 4)]
    zh_peers = [(y * Z_CHIPS + lax.rem(zh + k, 8) * 4 + zl, grp) for k in range(1, 8)]

    loads = [
        pltpu.make_async_copy(src, dst, in_sem.at[i])
        for i, (src, dst) in enumerate(
            [
                (prog.at[0], praw.at[0]),
                (prog.at[1], praw.at[1]),
                (wind, wraw),
                (slot, islot),
                (edge, iedge),
                (flip, iflip),
                (dest, idest),
                (wet, iwet),
            ]
        )
    ]
    for copy in loads:
        copy.start()

    barrier = pltpu.get_barrier_semaphore()
    peers = [(nxt, grp), (prv, grp)] + grp_peers + y_peers + zl_peers + zh_peers
    for peer in peers:
        pl.semaphore_signal(barrier, inc=1, device_id=peer, device_id_type=MESH)

    def pack(f):
        def body(k, carry):
            for n in range(16):
                at = pl.ds(pl.multiple_of(PLACE[n] * ELEMS + k * 8, 8), 8)
                p0[f, at, :] = praw[f, pl.ds(k * 128 + n, 8, stride=16), :]
            return carry

        lax.fori_loop(0, ELEMS // 8, body, 0)

    def halo(step, src, f):
        copies = []
        for way, target in enumerate((nxt, prv)):
            copies.append(
                pltpu.make_async_remote_copy(
                    src_ref=src.at[f, pl.ds(0, EDGE_ROWS)],
                    dst_ref=recv.at[step, f, pl.ds(way * EDGE_ROWS, EDGE_ROWS)],
                    send_sem=hs_sem.at[step, f, way],
                    recv_sem=hr_sem.at[step, f, way],
                    device_id=(target, grp),
                    device_id_type=MESH,
                )
            )
        return copies

    started = []
    halos = [[halo(s, src, f) for f in range(2)] for s, src in enumerate((p0, p1))]

    def send_halo(step, f):
        for copy in halos[step][f]:
            copy.start()
            started.append(copy)

    loads[0].wait()
    pack(0)
    pl.semaphore_wait(barrier, len(peers))
    send_halo(0, 0)
    loads[1].wait()
    pack(1)
    send_halo(0, 1)

    lane = lax.broadcasted_iota(jnp.int32, (8, LEV), 1)

    loads[2].wait()

    def count_body(k, total):
        at = pl.ds(pl.multiple_of(k * 32, 32), 32)
        speed = jnp.abs(wraw[0, at, :]) + jnp.abs(wraw[1, at, :])
        flag = jnp.where(speed > cfl_limit, 1.0, 0.0).astype(f32)
        return total + (flag[0:8] + flag[8:16] + flag[16:24] + flag[24:32])

    count = lax.fori_loop(0, ROWS // 32, count_body, jnp.zeros((8, LEV), f32))
    cval[0] = sum_rows(jnp.where(lane == 0, count, 0.0))

    stages = [(grp_peers, 0), (y_peers, 7), (zl_peers, 10), (zh_peers, 13)]

    def count_send(stage):
        targets, first = stages[stage]
        copies = []
        for k, peer in enumerate(targets):
            copy = pltpu.make_async_remote_copy(
                src_ref=cval.at[stage],
                dst_ref=crecv.at[first + k],
                send_sem=cs_sem.at[first + k],
                recv_sem=cr_sem.at[first + k],
                device_id=peer,
                device_id_type=MESH,
            )
            copy.start()
            copies.append(copy)
            started.append(copy)
        return copies

    def count_sum(stage, copies):
        for copy in copies:
            copy.wait_recv()
        targets, first = stages[stage]
        total = cval[stage]
        for k in range(len(targets)):
            total = total + crecv[first + k]
        return total

    flying = count_send(0)

    local_step(p0, wraw, base, 0)

    for copy in loads[3:]:
        copy.wait()
    s_, e_, f_ = islot[...], iedge[...], iflip[...]
    origin = jnp.where(s_ < ELEMS, 0, jnp.where(s_ < 2 * ELEMS, 2 * EDGE_ROWS, EDGE_ROWS))
    origin = origin + (s_ & (ELEMS - 1))
    facing = []
    for i in range(4):
        place = jnp.full(e_.shape, EDGE_PLACE[0][i], jnp.int32)
        for s in range(1, 4):
            place = jnp.where(e_ == s, EDGE_PLACE[s][i], place)
        facing.append(place)
    tq[...] = jnp.zeros_like(tq)
    for i in range(4):
        target = origin + ELEMS * jnp.where(f_ == 1, facing[3 - i], facing[i])
        low = target & (LEV - 1)
        tq[4 * i : 4 * i + 4, 0:ELEMS] = (target - low).astype(f32)
        tq[16 + 4 * i : 20 + 4 * i, 0:ELEMS] = low.astype(f32)
    wide = (32, 16 * LEV)
    pick = (lax.broadcasted_iota(jnp.int32, wide, 0) & 15) == (lax.broadcasted_iota(jnp.int32, wide, 1) >> 7)
    pick = jnp.where(pick, 1.0, 0.0).astype(bf16)
    bt[...] = lax.dot_general(
        tq[...].astype(bf16), pick, (((0,), (0,)), ((), ())), preferred_element_type=f32
    )[0:ELEMS]

    lanes32 = lax.broadcasted_iota(jnp.int32, (ELEMS, LEV), 1).astype(f32)

    def jm_body(k, carry):
        cell = lanes32 + (k * LEV).astype(f32)
        at = pl.ds(pl.multiple_of(k * LEV, LEV), LEV)
        for place in range(12):
            hit = None
            for s, i in SIDES[ORDER[place]]:
                col = (4 * i + s) * LEV
                one = jnp.where(bt[:, col : col + LEV] == cell, 1.0, 0.0)
                hit = one if hit is None else hit + one
            jm[place * ELEMS : (place + 1) * ELEMS, at] = hit.astype(bf16)
        return carry

    lax.fori_loop(0, 9, jm_body, 0)

    edge_scale = np.float32(time_step * penalty)

    def add_own(src, f):
        split_rows(src.at[f], rhs_own, EDGE_ROWS)
        got = jnp.dot(jm[:, 2 * EDGE_ROWS :], rhs_own[...], preferred_element_type=f32)
        base[f, 0:EDGE_ROWS, :] = base[f, 0:EDGE_ROWS, :] + edge_scale * (got[:, :LEV] + got[:, LEV:])

    def from_halo(step, f):
        for copy in halos[step][f]:
            copy.wait_recv()
        split_rows(recv.at[step, f], rhs, 2 * EDGE_ROWS)
        got = jnp.dot(jm[:, : 2 * EDGE_ROWS], rhs[...], preferred_element_type=f32)
        return edge_scale * (got[:, :LEV] + got[:, LEV:])

    add_own(p0, 0)
    total = count_sum(0, flying)
    cval[1] = total
    flying = count_send(1)
    local_step(p0, wraw, base, 1)
    add_own(p0, 1)

    row32 = lax.broadcasted_iota(jnp.int32, (8, LEV), 0)
    mine = (lane >> 4) == row32
    for j, ref in enumerate((iwet, idest)):
        for q in range(4):
            line = jnp.broadcast_to(ref[q : q + 1, :].astype(f32), (8, LEV))
            tq[8 * q : 8 * q + 8, :] = jnp.where(mine, line, 0.0)
        tall = (LEV, 16 * LEV)
        spread = (lax.broadcasted_iota(jnp.int32, tall, 0) & 15) == (lax.broadcasted_iota(jnp.int32, tall, 1) >> 7)
        spread = jnp.where(spread, 1.0, 0.0).astype(bf16)
        cols[j] = jnp.dot(tq[...].astype(bf16), spread, preferred_element_type=f32)

    for f in range(2):
        p1[f, 0:EDGE_ROWS, :] = base[f, 0:EDGE_ROWS, :] + from_halo(0, f)
        send_halo(1, f)
        p1[f, EDGE_ROWS:, :] = base[f, EDGE_ROWS:, :]
        if f == 0:
            total = count_sum(1, flying)
            cval[2] = total
            flying = count_send(2)
            local_step(p1, wraw, base, 0)
            add_own(p1, 0)
    local_step(p1, wraw, base, 1)
    add_own(p1, 1)
    total = count_sum(2, flying)
    cval[3] = total
    flying = count_send(3)

    stores = []

    def store(src, dst):
        copy = pltpu.make_async_copy(src, dst, out_sem.at[len(stores)])
        copy.start()
        stores.append(copy)

    def to_elements(src, dst, f, k):
        for n in range(16):
            at = pl.ds(pl.multiple_of(PLACE[n] * ELEMS + k * 8, 8), 8)
            dst[f, pl.ds(k * 128 + n, 8, stride=16), :] = src[f, at, :]

    for f in range(2):
        base[f, 0:EDGE_ROWS, :] = base[f, 0:EDGE_ROWS, :] + from_halo(1, f)

        def out_body(k, carry):
            to_elements(base, obuf, f, k)
            return carry

        lax.fori_loop(0, ELEMS // 8, out_body, 0)
        store(obuf.at[f], dyn.at[f])

    for place in range(16):
        at = slice(place * ELEMS, (place + 1) * ELEMS)
        warm, moist = base[0, at, :], base[1, at, :]
        active = cols[0, :, place_lanes(place)]
        x = 2.0 * (moist - 0.5 * jnp.exp(0.3 * warm))
        soft = jnp.maximum(x, 0.0) + jnp.log1p(jnp.exp(-jnp.abs(x)))
        condense = jnp.where(lanes32 < active, 0.5 * soft, 0.0)
        high = condense.astype(bf16)
        condf[at, :] = condense
        cond[at, 0:LEV] = high
        cond[at, LEV:] = (condense - high.astype(f32)).astype(bf16)
    deep = (2 * LEV, LEV)
    above = (lax.broadcasted_iota(jnp.int32, deep, 0) & (LEV - 1)) > lax.broadcasted_iota(jnp.int32, deep, 1)
    above = jnp.where(above, 1.0, 0.0).astype(bf16)
    flux = jnp.dot(cond[...], above, preferred_element_type=f32)
    sums = [jnp.zeros((8, LEV), f32) for _ in range(8)]
    for place in range(16):
        at = slice(place * ELEMS, (place + 1) * ELEMS)
        n = ORDER[place]
        active = cols[0, :, place_lanes(place)]
        owner = cols[1, :, place_lanes(place)]
        condense = condf[at, :]
        net = condense - jnp.where(lanes32 < active, evap_rate * flux[at, :], 0.0)
        warming, drying = latent * net, -net
        for k in range(4):
            spot = pl.ds(k * 128 + n, 8, stride=16)
            tbuf[0, spot, :] = warming[8 * k : 8 * k + 8]
            tbuf[1, spot, :] = drying[8 * k : 8 * k + 8]
        for g in range(8):
            share = jnp.where(owner == float(g), net, 0.0)
            sums[g] = sums[g] + (share[0:8] + share[8:16] + share[16:24] + share[24:32])
    for g in range(8):
        part[g] = sum_rows(sums[g])
    rain_copies = []
    for k, (_, peer) in enumerate(grp_peers):
        copy = pltpu.make_async_remote_copy(
            src_ref=part.at[peer],
            dst_ref=precv.at[k],
            send_sem=rs_sem.at[k],
            recv_sem=rr_sem.at[k],
            device_id=(me, peer),
            device_id_type=MESH,
        )
        copy.start()
        rain_copies.append(copy)
        started.append(copy)
    store(tbuf, tend)

    cfl[0] = jnp.sum(count_sum(3, flying))
    for copy in rain_copies:
        copy.wait_recv()
    collected = part[grp]
    for k in range(7):
        collected = collected + precv[k]
    rain[0] = jnp.sum(collected) * np.float32(1.0 / ROWS)
    for copy in started:
        copy.wait_send()
    for copy in stores:
        copy.wait()


def place_lanes(place):
    n = ORDER[place]
    return slice(n * LEV, (n + 1) * LEV)


def shards(prognostic, wind_field, nbr_slot, nbr_edge, flip_edge, span_dest, wet_layers_present):
    f32 = jnp.float32
    anywhere = pl.BlockSpec(memory_space=pl.ANY)
    scalar = pl.BlockSpec(memory_space=pltpu.SMEM)
    vmem = pltpu.VMEM
    dma = pltpu.SemaphoreType.DMA
    whole = (2, ROWS, LEV)
    fields, tendency, rain, cfl = pl.pallas_call(
        kernel,
        out_shape=(
            jax.ShapeDtypeStruct(whole, f32),
            jax.ShapeDtypeStruct(whole, f32),
            jax.ShapeDtypeStruct((1,), f32),
            jax.ShapeDtypeStruct((1,), f32),
        ),
        in_specs=[anywhere] * 7,
        out_specs=(anywhere, anywhere, scalar, scalar),
        scratch_shapes=[
            vmem(whole, f32),
            vmem(whole, f32),
            vmem((4, ELEMS), jnp.int32),
            vmem((4, ELEMS), jnp.int32),
            vmem((4, ELEMS), jnp.int32),
            vmem((4, LEV), jnp.int32),
            vmem((4, LEV), jnp.int32),
            vmem(whole, f32),
            vmem(whole, f32),
            vmem(whole, f32),
            vmem((2, 2, 2 * EDGE_ROWS, LEV), f32),
            vmem((EDGE_ROWS, 3 * EDGE_ROWS), jnp.bfloat16),
            vmem((2 * EDGE_ROWS, 2 * LEV), jnp.bfloat16),
            vmem((EDGE_ROWS, 2 * LEV), jnp.bfloat16),
            vmem((ELEMS, LEV), f32),
            vmem((ELEMS, 16 * LEV), f32),
            vmem((2, ELEMS, 16 * LEV), f32),
            vmem((ROWS, 2 * LEV), jnp.bfloat16),
            vmem((ROWS, LEV), f32),
            vmem(whole, f32),
            vmem(whole, f32),
            vmem((4, 1, LEV), f32),
            vmem((20, 1, LEV), f32),
            vmem((8, 1, LEV), f32),
            vmem((7, 1, LEV), f32),
            dma((8,)),
            dma((2, 2, 2)),
            dma((2, 2, 2)),
            dma((20,)),
            dma((20,)),
            dma((7,)),
            dma((7,)),
            dma((3,)),
        ],
        compiler_params=pltpu.CompilerParams(
            collective_id=0, has_side_effects=True, vmem_limit_bytes=48 * 1024 * 1024
        ),
        cost_estimate=pl.CostEstimate(flops=2_000_000_000, bytes_accessed=2_200_000, transcendentals=200_000),
        name="steps_and_columns",
    )(
        prognostic.reshape(whole),
        wind_field.reshape(whole),
        nbr_slot.T,
        nbr_edge.T,
        flip_edge.T,
        span_dest.reshape(4, LEV),
        wet_layers_present.reshape(4, LEV),
    )
    shape = prognostic.shape
    return fields.reshape(shape), tendency.reshape(shape), rain, cfl.reshape(())


def solution(mesh):
    in_specs = (
        P(None, ("elem", "grp"), None, None),
        P(None, ("elem", "grp"), None, None),
        P(("elem", "grp"), None),
        P(("elem", "grp"), None),
        P(("elem", "grp"), None),
        P(("elem", "grp"), None),
        P(("elem", "grp")),
    )
    out_specs = (
        P(None, ("elem", "grp"), None, None),
        P(None, ("elem", "grp"), None, None),
        P(("elem", "grp")),
        P(),
    )
    return jax.shard_map(shards, mesh=mesh, in_specs=in_specs, out_specs=out_specs, check_vma=False)
```

```python
import math

import jax
import jax.numpy as jnp
import numpy as np
from jax import lax
from jax.experimental import pallas as pl
from jax.experimental.pallas import tpu as pltpu
from jax.sharding import PartitionSpec as P

STEPS = 2
ELEMS = 32
ROWS = 512
LEV = 128
EDGE_ROWS = 384

edge_nodes = np.array([[0, 1, 2, 3], [3, 7, 11, 15], [12, 13, 14, 15], [0, 4, 8, 12]])
time_step = 0.02
viscosity = 0.05
penalty = 4.0
cfl_limit = 2.0
latent = 1.5
evap_rate = 0.02

ORDER = [0, 1, 2, 3, 4, 7, 8, 11, 12, 13, 14, 15, 5, 6, 9, 10]
PLACE = {n: p for p, n in enumerate(ORDER)}
EDGE_PLACE = [[PLACE[int(n)] for n in nodes] for nodes in edge_nodes]
SIDES = {n: [(s, i) for s in range(4) for i in range(4) if edge_nodes[s][i] == n] for n in range(16)}

Z_CHIPS = 32
ROOT = 4
MESH = pl.DeviceIdType.MESH


def nodal_derivative_matrix():
    points = np.array([-1.0, -1.0 / math.sqrt(5.0), 1.0 / math.sqrt(5.0), 1.0])
    off_diag = points[:, None] - points[None, :] + np.eye(4)
    weights = 1.0 / np.prod(off_diag, axis=1)
    derivative = weights[None, :] / weights[:, None] / off_diag
    derivative = derivative * (1.0 - np.eye(4))
    return derivative - np.eye(4) * np.sum(derivative, axis=1)[:, None]


D1 = nodal_derivative_matrix()
D2 = D1 @ D1


def weighted(coefs, values):
    total = None
    for coef, value in zip(coefs, values):
        if abs(coef) < 1e-12:
            continue
        term = value * np.float32(coef)
        total = term if total is None else total + term
    return total


def split_rows(src, dst, rows):
    step = 64

    def body(k, carry):
        at = pl.ds(pl.multiple_of(k * step, step), step)
        x = src[at, :]
        high = x.astype(jnp.bfloat16)
        dst[at, 0:LEV] = high
        dst[at, LEV : 2 * LEV] = (x - high.astype(jnp.float32)).astype(jnp.bfloat16)
        return carry

    lax.fori_loop(0, rows // step, body, 0)


def local_step(src, wind, base, f):
    def body(k, carry):
        at = lambda n: pl.ds(pl.multiple_of(PLACE[n] * ELEMS + k * 8, 8), 8)
        F = [src[f, at(n), :] for n in range(16)]
        for n in range(16):
            r, c = divmod(n, 4)
            row = [F[4 * r + b] for b in range(4)]
            col = [F[4 * b + c] for b in range(4)]
            u = wind[0, pl.ds(k * 128 + n, 8, stride=16), :]
            v = wind[1, pl.ds(k * 128 + n, 8, stride=16), :]
            grad_col = weighted(D1[c] * -time_step, row)
            grad_row = weighted(D1[r] * -time_step, col)
            centre = 1.0 - time_step * penalty * len(SIDES[n])
            centre = centre + time_step * viscosity * (D2[c][c] + D2[r][r])
            others = [b for b in range(4) if b != c]
            others_r = [b for b in range(4) if b != r]
            lap = weighted(
                [centre]
                + [time_step * viscosity * D2[c][b] for b in others]
                + [time_step * viscosity * D2[r][b] for b in others_r],
                [F[n]] + [row[b] for b in others] + [col[b] for b in others_r],
            )
            base[f, at(n), :] = lap + u * grad_col + v * grad_row
        return carry

    lax.fori_loop(0, ELEMS // 8, body, 0)


def sum_rows(x):
    return jnp.sum(x, axis=0, keepdims=True)


def kernel(
    prog, wind, slot, edge, flip, dest, wet,
    dyn, tend, sums_out,
    praw, wraw, islot, iedge, iflip, idest, iwet,
    p0, p1, base, recv, jm, rhs, rhs_own, tq, bt, cols, cond, condf, obuf, tbuf,
    cval, crecv, gsum, ctot, part, precv, lines,
    in_sem, hs_sem, hr_sem, cs_sem, cr_sem, gs_sem, gr_sem, rs_sem, rr_sem, out_sem,
):
    f32, bf16 = jnp.float32, jnp.bfloat16
    me = lax.axis_index("elem")
    grp = lax.axis_index("grp")
    n_elem = lax.axis_size("elem")
    nxt, prv = lax.rem(me + 1, n_elem), lax.rem(me + n_elem - 1, n_elem)
    y, z = me // Z_CHIPS, lax.rem(me, Z_CHIPS)
    grp_peers = [(me, lax.rem(grp + k, 8)) for k in range(1, 8)]
    z_line = [(y * Z_CHIPS + lax.rem(ROOT + k, Z_CHIPS), grp) for k in range(1, Z_CHIPS)]
    away = lax.rem(z + Z_CHIPS - ROOT, Z_CHIPS)
    is_root = z == ROOT

    halves = lambda src, dst: [(src.at[pl.ds(k, 256)], dst.at[pl.ds(k, 256)]) for k in (0, 256)]
    pieces = halves(prog.at[0], praw.at[0])
    pieces += halves(wind.at[0], wraw.at[0]) + halves(wind.at[1], wraw.at[1])
    pieces += halves(prog.at[1], praw.at[1])
    pieces += [(slot, islot), (edge, iedge), (flip, iflip), (dest, idest), (wet, iwet)]
    loads = [pltpu.make_async_copy(src, dst, in_sem.at[i]) for i, (src, dst) in enumerate(pieces)]
    for copy in loads:
        copy.start()

    barrier = pltpu.get_barrier_semaphore()

    def greet(peer):
        pl.semaphore_signal(barrier, inc=1, device_id=peer, device_id_type=MESH)

    for peer in [(nxt, grp), (prv, grp)] + grp_peers:
        greet(peer)

    @pl.when(is_root)
    def _():
        def greet_body(k, carry):
            greet((lax.rem(y + k // Z_CHIPS, 4) * Z_CHIPS + lax.rem(ROOT + lax.rem(k, Z_CHIPS), Z_CHIPS), grp))
            return carry

        lax.fori_loop(1, 4 * Z_CHIPS, greet_body, 0)

    def pack(f):
        def body(k, carry):
            for n in range(16):
                at = pl.ds(pl.multiple_of(PLACE[n] * ELEMS + k * 8, 8), 8)
                p0[f, at, :] = praw[f, pl.ds(k * 128 + n, 8, stride=16), :]
            return carry

        lax.fori_loop(0, ELEMS // 8, body, 0)

    def halo(step, src, f):
        copies = []
        for way, target in enumerate((nxt, prv)):
            copies.append(
                pltpu.make_async_remote_copy(
                    src_ref=src.at[f, pl.ds(0, EDGE_ROWS)],
                    dst_ref=recv.at[step, f, pl.ds(way * EDGE_ROWS, EDGE_ROWS)],
                    send_sem=hs_sem.at[step, f, way],
                    recv_sem=hr_sem.at[step, f, way],
                    device_id=(target, grp),
                    device_id_type=MESH,
                )
            )
        return copies

    started = []
    halos = [[halo(s, src, f) for f in range(2)] for s, src in enumerate((p0, p1))]

    def send_halo(step, f):
        for copy in halos[step][f]:
            copy.start()
            started.append(copy)

    def arrived(first, last):
        for copy in loads[first:last]:
            copy.wait()

    arrived(2, 6)
    lane = lax.broadcasted_iota(jnp.int32, (8, LEV), 1)

    def count_body(k, total):
        at = pl.ds(pl.multiple_of(k * 32, 32), 32)
        speed = jnp.abs(wraw[0, at, :]) + jnp.abs(wraw[1, at, :])
        flag = jnp.where(speed > cfl_limit, 1.0, 0.0).astype(f32)
        return total + (flag[0:8] + flag[8:16] + flag[16:24] + flag[24:32])

    count = lax.fori_loop(0, ROWS // 32, count_body, jnp.zeros((8, LEV), f32))
    cval[0] = sum_rows(jnp.where(lane == 0, count, 0.0))
    crecv[0] = cval[0]

    def remote(src, dst, send_sem, recv_sem, peer):
        return pltpu.make_async_remote_copy(
            src_ref=src, dst_ref=dst, send_sem=send_sem, recv_sem=recv_sem, device_id=peer, device_id_type=MESH
        )

    to_root = [
        remote(
            cval.at[0],
            crecv.at[(4 - j) % 4 * Z_CHIPS + away],
            cs_sem.at[j],
            cr_sem.at[0],
            (lax.rem(y + j, 4) * Z_CHIPS + ROOT, grp),
        )
        for j in range(4)
    ]

    arrived(0, 2)
    pack(0)
    pl.semaphore_wait(barrier, jnp.where(is_root, 12, 13))

    @pl.when(z != ROOT)
    def _():
        to_root[0].start()

    for copy in to_root[1:]:
        copy.start()
    started.extend(to_root[1:])
    send_halo(0, 0)
    arrived(6, 8)
    pack(1)
    send_halo(0, 1)

    local_step(p0, wraw, base, 0)

    arrived(8, 13)
    s_, e_, f_ = islot[...], iedge[...], iflip[...]
    origin = jnp.where(s_ < ELEMS, 0, jnp.where(s_ < 2 * ELEMS, 2 * EDGE_ROWS, EDGE_ROWS))
    origin = origin + (s_ & (ELEMS - 1))
    facing = []
    for i in range(4):
        place = jnp.full(e_.shape, EDGE_PLACE[0][i], jnp.int32)
        for s in range(1, 4):
            place = jnp.where(e_ == s, EDGE_PLACE[s][i], place)
        facing.append(place)
    tq[...] = jnp.zeros_like(tq)
    for i in range(4):
        target = origin + ELEMS * jnp.where(f_ == 1, facing[3 - i], facing[i])
        low = target & (LEV - 1)
        tq[4 * i : 4 * i + 4, 0:ELEMS] = (target - low).astype(f32)
        tq[16 + 4 * i : 20 + 4 * i, 0:ELEMS] = low.astype(f32)
    wide = (32, 16 * LEV)
    pick = (lax.broadcasted_iota(jnp.int32, wide, 0) & 15) == (lax.broadcasted_iota(jnp.int32, wide, 1) >> 7)
    pick = jnp.where(pick, 1.0, 0.0).astype(bf16)
    bt[...] = lax.dot_general(
        tq[...].astype(bf16), pick, (((0,), (0,)), ((), ())), preferred_element_type=f32
    )[0:ELEMS]

    lanes32 = lax.broadcasted_iota(jnp.int32, (ELEMS, LEV), 1).astype(f32)

    def jm_body(k, carry):
        cell = lanes32 + (k * LEV).astype(f32)
        at = pl.ds(pl.multiple_of(k * LEV, LEV), LEV)
        for place in range(12):
            hit = None
            for s, i in SIDES[ORDER[place]]:
                col = (4 * i + s) * LEV
                one = jnp.where(bt[:, col : col + LEV] == cell, 1.0, 0.0)
                hit = one if hit is None else hit + one
            jm[place * ELEMS : (place + 1) * ELEMS, at] = hit.astype(bf16)
        return carry

    lax.fori_loop(0, 9, jm_body, 0)

    edge_scale = np.float32(time_step * penalty)

    def add_own(src, f):
        split_rows(src.at[f], rhs_own, EDGE_ROWS)
        got = jnp.dot(jm[:, 2 * EDGE_ROWS :], rhs_own[...], preferred_element_type=f32)
        base[f, 0:EDGE_ROWS, :] = base[f, 0:EDGE_ROWS, :] + edge_scale * (got[:, :LEV] + got[:, LEV:])

    def from_halo(step, f):
        for copy in halos[step][f]:
            copy.wait_recv()
        split_rows(recv.at[step, f], rhs, 2 * EDGE_ROWS)
        got = jnp.dot(jm[:, : 2 * EDGE_ROWS], rhs[...], preferred_element_type=f32)
        return edge_scale * (got[:, :LEV] + got[:, LEV:])

    add_own(p0, 0)
    local_step(p0, wraw, base, 1)
    add_own(p0, 1)

    row32 = lax.broadcasted_iota(jnp.int32, (8, LEV), 0)
    mine = (lane >> 4) == row32
    for j, ref in enumerate((iwet, idest)):
        for q in range(4):
            line = jnp.broadcast_to(ref[q : q + 1, :].astype(f32), (8, LEV))
            tq[8 * q : 8 * q + 8, :] = jnp.where(mine, line, 0.0)
        tall = (LEV, 16 * LEV)
        spread = (lax.broadcasted_iota(jnp.int32, tall, 0) & 15) == (lax.broadcasted_iota(jnp.int32, tall, 1) >> 7)
        spread = jnp.where(spread, 1.0, 0.0).astype(bf16)
        cols[j] = jnp.dot(tq[...].astype(bf16), spread, preferred_element_type=f32)

    for f in range(2):
        p1[f, 0:EDGE_ROWS, :] = base[f, 0:EDGE_ROWS, :] + from_halo(0, f)
        send_halo(1, f)
        p1[f, EDGE_ROWS:, :] = base[f, EDGE_ROWS:, :]
        if f == 0:
            local_step(p1, wraw, base, 0)
            add_own(p1, 0)
    local_step(p1, wraw, base, 1)
    add_own(p1, 1)

    stores = []

    def store(src, dst):
        copy = pltpu.make_async_copy(src, dst, out_sem.at[len(stores)])
        copy.start()
        stores.append(copy)

    def to_elements(src, dst, f, k):
        for n in range(16):
            at = pl.ds(pl.multiple_of(PLACE[n] * ELEMS + k * 8, 8), 8)
            dst[f, pl.ds(k * 128 + n, 8, stride=16), :] = src[f, at, :]

    def out_field(f):
        def body(k, carry):
            to_elements(base, obuf, f, k)
            return carry

        lax.fori_loop(0, ELEMS // 8, body, 0)
        store(obuf.at[f], dyn.at[f])

    base[0, 0:EDGE_ROWS, :] = base[0, 0:EDGE_ROWS, :] + from_halo(1, 0)
    out_field(0)

    def threshold(k, carry):
        at = pl.ds(pl.multiple_of(k * 32, 32), 32)
        condf[at, :] = jnp.exp(0.3 * base[0, at, :])
        return carry

    lax.fori_loop(0, ROWS // 32, threshold, 0)
    base[1, 0:EDGE_ROWS, :] = base[1, 0:EDGE_ROWS, :] + from_halo(1, 1)

    for place in range(16):
        at = slice(place * ELEMS, (place + 1) * ELEMS)
        active = cols[0, :, place_lanes(place)]
        x = 2.0 * base[1, at, :] - condf[at, :]
        soft = jnp.maximum(x, 0.0) + jnp.log1p(jnp.exp(-jnp.abs(x)))
        condense = jnp.where(lanes32 < active, 0.5 * soft, 0.0)
        high = condense.astype(bf16)
        condf[at, :] = condense
        cond[at, 0:LEV] = high
        cond[at, LEV:] = (condense - high.astype(f32)).astype(bf16)
    deep = (2 * LEV, LEV)
    above = (lax.broadcasted_iota(jnp.int32, deep, 0) & (LEV - 1)) > lax.broadcasted_iota(jnp.int32, deep, 1)
    above = jnp.where(above, 1.0, 0.0).astype(bf16)
    flux = jnp.dot(cond[...], above, preferred_element_type=f32)
    sums = [jnp.zeros((8, LEV), f32) for _ in range(8)]
    for place in range(16):
        at = slice(place * ELEMS, (place + 1) * ELEMS)
        active = cols[0, :, place_lanes(place)]
        owner = cols[1, :, place_lanes(place)]
        condense = condf[at, :]
        net = condense - jnp.where(lanes32 < active, evap_rate * flux[at, :], 0.0)
        condf[at, :] = net
        for g in range(8):
            share = jnp.where(owner == float(g), net, 0.0)
            sums[g] = sums[g] + (share[0:8] + share[8:16] + share[16:24] + share[24:32])
    for g in range(8):
        part[g] = sum_rows(sums[g])
    rain_copies = []
    for k, (_, peer) in enumerate(grp_peers):
        copy = pltpu.make_async_remote_copy(
            src_ref=part.at[peer],
            dst_ref=precv.at[k],
            send_sem=rs_sem.at[k],
            recv_sem=rr_sem.at[k],
            device_id=(me, peer),
            device_id_type=MESH,
        )
        copy.start()
        rain_copies.append(copy)
        started.append(copy)
    out_field(1)

    def tend_body(k, carry):
        for n in range(16):
            at = pl.ds(pl.multiple_of(PLACE[n] * ELEMS + k * 8, 8), 8)
            spot = pl.ds(k * 128 + n, 8, stride=16)
            net = condf[at, :]
            tbuf[0, spot, :] = latent * net
            tbuf[1, spot, :] = -net
        return carry

    lax.fori_loop(0, ELEMS // 8, tend_body, 0)
    store(tbuf, tend)

    for copy in rain_copies:
        copy.wait_recv()
    collected = part[grp]
    for k in range(7):
        collected = collected + precv[k]
    lines[0] = collected * np.float32(1.0 / ROWS)

    over_grp = [remote(cval.at[1], gsum.at[k], gs_sem.at[k], gr_sem.at[k], peer) for k, peer in enumerate(grp_peers)]
    back = [remote(cval.at[2], ctot.at[0], gs_sem.at[6 + k], cr_sem.at[1], peer) for k, peer in enumerate(z_line, 1)]

    @pl.when(is_root)
    def _():
        rest = crecv.at[pl.ds(1, 4 * Z_CHIPS - 1)]
        remote(rest, rest, cs_sem.at[0], cr_sem.at[0], (nxt, grp)).wait_recv()
        total = jnp.sum(crecv[...], axis=0)
        cval[1] = total
        for copy in over_grp:
            copy.start()
        for copy in over_grp:
            copy.wait_recv()
        total = total + jnp.sum(gsum[...], axis=0)
        cval[2] = total
        for copy in back:
            copy.start()
        ctot[0] = total
        for copy in over_grp + back:
            copy.wait_send()

    @pl.when(z != ROOT)
    def _():
        back[0].wait_recv()
        to_root[0].wait_send()

    lines[1] = ctot[0]
    store(lines, sums_out)
    for copy in started:
        copy.wait_send()
    for copy in stores:
        copy.wait()


def place_lanes(place):
    n = ORDER[place]
    return slice(n * LEV, (n + 1) * LEV)


def hand_over(dyn, tend, sums, dyn_out, tend_out, rain_out, cfl_out, lines, sem):
    small = pltpu.make_async_copy(sums, lines, sem.at[8])
    small.start()
    copies = []
    for src, dst in ((dyn, dyn_out), (tend, tend_out)):
        for f in range(2):
            for k in range(2):
                at = pl.ds(k * 256, 256)
                copies.append(pltpu.make_async_copy(src.at[f, at], dst.at[f, at], sem.at[len(copies)]))
                copies[-1].start()
    small.wait()
    rain_out[0] = jnp.sum(lines[0])
    cfl_out[0] = jnp.sum(lines[1])
    for copy in copies:
        copy.wait()


def shards(prognostic, wind_field, nbr_slot, nbr_edge, flip_edge, span_dest, wet_layers_present):
    f32 = jnp.float32
    anywhere = pl.BlockSpec(memory_space=pl.ANY)
    scalar = pl.BlockSpec(memory_space=pltpu.SMEM)
    vmem = pltpu.VMEM
    dma = pltpu.SemaphoreType.DMA
    whole = (2, ROWS, LEV)
    fields, tendency, sums = pl.pallas_call(
        kernel,
        out_shape=(
            jax.ShapeDtypeStruct(whole, f32),
            jax.ShapeDtypeStruct(whole, f32),
            jax.ShapeDtypeStruct((2, 1, LEV), f32),
        ),
        in_specs=[pl.BlockSpec(memory_space=pltpu.HBM)] * 7,
        out_specs=(anywhere, anywhere, anywhere),
        scratch_shapes=[
            vmem(whole, f32),
            vmem(whole, f32),
            vmem((4, ELEMS), jnp.int32),
            vmem((4, ELEMS), jnp.int32),
            vmem((4, ELEMS), jnp.int32),
            vmem((4, LEV), jnp.int32),
            vmem((4, LEV), jnp.int32),
            vmem(whole, f32),
            vmem(whole, f32),
            vmem(whole, f32),
            vmem((2, 2, 2 * EDGE_ROWS, LEV), f32),
            vmem((EDGE_ROWS, 3 * EDGE_ROWS), jnp.bfloat16),
            vmem((2 * EDGE_ROWS, 2 * LEV), jnp.bfloat16),
            vmem((EDGE_ROWS, 2 * LEV), jnp.bfloat16),
            vmem((ELEMS, LEV), f32),
            vmem((ELEMS, 16 * LEV), f32),
            vmem((2, ELEMS, 16 * LEV), f32),
            vmem((ROWS, 2 * LEV), jnp.bfloat16),
            vmem((ROWS, LEV), f32),
            vmem(whole, f32),
            vmem(whole, f32),
            vmem((3, 1, LEV), f32),
            vmem((4 * Z_CHIPS, 1, LEV), f32),
            vmem((7, 1, LEV), f32),
            vmem((1, 1, LEV), f32),
            vmem((8, 1, LEV), f32),
            vmem((7, 1, LEV), f32),
            vmem((2, 1, LEV), f32),
            dma((13,)),
            dma((2, 2, 2)),
            dma((2, 2, 2)),
            dma((4,)),
            dma((2,)),
            dma((38,)),
            dma((7,)),
            dma((7,)),
            dma((7,)),
            dma((4,)),
        ],
        compiler_params=pltpu.CompilerParams(
            collective_id=0, has_side_effects=True, vmem_limit_bytes=52 * 1024 * 1024 + 655360
        ),
        cost_estimate=pl.CostEstimate(flops=2_000_000_000, bytes_accessed=2_200_000, transcendentals=200_000),
        name="steps_and_columns",
    )(
        prognostic.reshape(whole),
        wind_field.reshape(whole),
        nbr_slot.T,
        nbr_edge.T,
        flip_edge.T,
        span_dest.reshape(4, LEV),
        wet_layers_present.reshape(4, LEV),
    )
    fields, tendency, rain, cfl = pl.pallas_call(
        hand_over,
        out_shape=(
            jax.ShapeDtypeStruct(whole, f32),
            jax.ShapeDtypeStruct(whole, f32),
            jax.ShapeDtypeStruct((1,), f32),
            jax.ShapeDtypeStruct((1,), f32),
        ),
        in_specs=[anywhere, anywhere, anywhere],
        out_specs=(anywhere, anywhere, scalar, scalar),
        scratch_shapes=[vmem((2, 1, LEV), f32), dma((9,))],
        compiler_params=pltpu.CompilerParams(vmem_limit_bytes=6 * 1024 * 1024),
        name="hand_over",
    )(fields, tendency, sums)
    shape = prognostic.shape
    return fields.reshape(shape), tendency.reshape(shape), rain, cfl.reshape(())


def solution(mesh):
    in_specs = (
        P(None, ("elem", "grp"), None, None),
        P(None, ("elem", "grp"), None, None),
        P(("elem", "grp"), None),
        P(("elem", "grp"), None),
        P(("elem", "grp"), None),
        P(("elem", "grp"), None),
        P(("elem", "grp")),
    )
    out_specs = (
        P(None, ("elem", "grp"), None, None),
        P(None, ("elem", "grp"), None, None),
        P(("elem", "grp")),
        P(),
    )
    return jax.shard_map(shards, mesh=mesh, in_specs=in_specs, out_specs=out_specs, check_vma=False)
```

```python
import math

import jax
import jax.numpy as jnp
import numpy as np
from jax import lax
from jax.experimental import pallas as pl
from jax.experimental.pallas import tpu as pltpu
from jax.sharding import PartitionSpec as P

STEPS = 2
ELEMS = 32
ROWS = 512
LEV = 128
EDGE_ROWS = 384
PARTS = ((0, 256), (256, 128))

edge_nodes = np.array([[0, 1, 2, 3], [3, 7, 11, 15], [12, 13, 14, 15], [0, 4, 8, 12]])
time_step = 0.02
viscosity = 0.05
penalty = 4.0
cfl_limit = 2.0
latent = 1.5
evap_rate = 0.02

ORDER = [0, 1, 2, 3, 4, 7, 8, 11, 12, 13, 14, 15, 5, 6, 9, 10]
PLACE = {n: p for p, n in enumerate(ORDER)}
EDGE_PLACE = [[PLACE[int(n)] for n in nodes] for nodes in edge_nodes]
SIDES = {n: [(s, i) for s in range(4) for i in range(4) if edge_nodes[s][i] == n] for n in range(16)}

Z_CHIPS = 32
ROOT = 3
MESH = pl.DeviceIdType.MESH


def nodal_derivative_matrix():
    points = np.array([-1.0, -1.0 / math.sqrt(5.0), 1.0 / math.sqrt(5.0), 1.0])
    off_diag = points[:, None] - points[None, :] + np.eye(4)
    weights = 1.0 / np.prod(off_diag, axis=1)
    derivative = weights[None, :] / weights[:, None] / off_diag
    derivative = derivative * (1.0 - np.eye(4))
    return derivative - np.eye(4) * np.sum(derivative, axis=1)[:, None]


D1 = nodal_derivative_matrix()
D2 = D1 @ D1


def weighted(coefs, values):
    total = None
    for coef, value in zip(coefs, values):
        if abs(coef) < 1e-12:
            continue
        term = value * np.float32(coef)
        total = term if total is None else total + term
    return total


def split_rows(src, dst, rows, first=0):
    step = 64

    def body(k, carry):
        at = pl.ds(pl.multiple_of(first + k * step, step), step)
        x = src[at, :]
        high = x.astype(jnp.bfloat16)
        dst[at, 0:LEV] = high
        dst[at, LEV : 2 * LEV] = (x - high.astype(jnp.float32)).astype(jnp.bfloat16)
        return carry

    lax.fori_loop(0, rows // step, body, 0)


def local_step(src, wind, base, f):
    def body(k, carry):
        at = lambda n: pl.ds(pl.multiple_of(PLACE[n] * ELEMS + k * 8, 8), 8)
        F = [src[f, at(n), :] for n in range(16)]
        for n in range(16):
            r, c = divmod(n, 4)
            row = [F[4 * r + b] for b in range(4)]
            col = [F[4 * b + c] for b in range(4)]
            u = wind[0, pl.ds(k * 128 + n, 8, stride=16), :]
            v = wind[1, pl.ds(k * 128 + n, 8, stride=16), :]
            grad_col = weighted(D1[c] * -time_step, row)
            grad_row = weighted(D1[r] * -time_step, col)
            centre = 1.0 - time_step * penalty * len(SIDES[n])
            centre = centre + time_step * viscosity * (D2[c][c] + D2[r][r])
            others = [b for b in range(4) if b != c]
            others_r = [b for b in range(4) if b != r]
            lap = weighted(
                [centre]
                + [time_step * viscosity * D2[c][b] for b in others]
                + [time_step * viscosity * D2[r][b] for b in others_r],
                [F[n]] + [row[b] for b in others] + [col[b] for b in others_r],
            )
            base[f, at(n), :] = lap + u * grad_col + v * grad_row
        return carry

    lax.fori_loop(0, ELEMS // 8, body, 0)


def sum_rows(x):
    return jnp.sum(x, axis=0, keepdims=True)


def kernel(
    prog, wind, slot, edge, flip, dest, wet,
    dyn, tend, sums_out,
    praw, wraw, islot, iedge, iflip, idest, iwet,
    p0, p1, base, recv, jm, rhs, rhs_own, tq, bt, cols, cond, condf, obuf, tbuf,
    cval, crecv, gsum, ctot, part, precv, lines,
    in_sem, hs_sem, hr_sem, cs_sem, cr_sem, gs_sem, gr_sem, rs_sem, rr_sem, out_sem, word_sem,
):
    f32, bf16 = jnp.float32, jnp.bfloat16
    me = lax.axis_index("elem")
    grp = lax.axis_index("grp")
    n_elem = lax.axis_size("elem")
    nxt, prv = lax.rem(me + 1, n_elem), lax.rem(me + n_elem - 1, n_elem)
    y, z = me // Z_CHIPS, lax.rem(me, Z_CHIPS)
    grp_peers = [(me, lax.rem(grp + k, 8)) for k in range(1, 8)]
    z_line = [(y * Z_CHIPS + lax.rem(ROOT + k, Z_CHIPS), grp) for k in range(1, Z_CHIPS)]
    away = lax.rem(z + Z_CHIPS - ROOT, Z_CHIPS)
    is_root = z == ROOT

    halves = lambda src, dst: [(src.at[pl.ds(k, 256)], dst.at[pl.ds(k, 256)]) for k in (0, 256)]
    pieces = halves(prog.at[0], praw.at[0])
    pieces += halves(wind.at[0], wraw.at[0]) + halves(wind.at[1], wraw.at[1])
    pieces += halves(prog.at[1], praw.at[1])
    pieces += [(slot, islot), (edge, iedge), (flip, iflip), (dest, idest), (wet, iwet)]
    loads = [pltpu.make_async_copy(src, dst, in_sem.at[i]) for i, (src, dst) in enumerate(pieces)]
    for copy in loads:
        copy.start()

    barrier = pltpu.get_barrier_semaphore()

    def greet(peer):
        pl.semaphore_signal(barrier, inc=1, device_id=peer, device_id_type=MESH)

    near = [(me, lax.rem(grp + 2 * i, 8)) for i in (1, 3)]
    core = lax.rem(grp, 2)
    near += [(me, lax.rem(grp - core + 2 * i, 8) + 1 - core) for i in (0, 1, 3)]
    for peer in [(nxt, grp), (prv, grp)] + near:
        greet(peer)

    @pl.when(is_root)
    def _():
        def greet_body(k, carry):
            greet((lax.rem(y + k // Z_CHIPS, 4) * Z_CHIPS + lax.rem(ROOT + lax.rem(k, Z_CHIPS), Z_CHIPS), grp))
            return carry

        lax.fori_loop(1, 4 * Z_CHIPS, greet_body, 0)

    def pack(f):
        def body(k, carry):
            for n in range(16):
                at = pl.ds(pl.multiple_of(PLACE[n] * ELEMS + k * 8, 8), 8)
                p0[f, at, :] = praw[f, pl.ds(k * 128 + n, 8, stride=16), :]
            return carry

        lax.fori_loop(0, ELEMS // 8, body, 0)

    def halo(step, src, f, part):
        first, rows = PARTS[part]
        return [
            pltpu.make_async_remote_copy(
                src_ref=src.at[f, pl.ds(first, rows)],
                dst_ref=recv.at[step, f, pl.ds(2 * first + way * rows, rows)],
                send_sem=hs_sem.at[step, f, 2 * part + way],
                recv_sem=hr_sem.at[step, f, 2 * part + way],
                device_id=(target, grp),
                device_id_type=MESH,
            )
            for way, target in enumerate((nxt, prv))
        ]

    started = []
    halos = [[[halo(s, src, f, p) for p in range(2)] for f in range(2)] for s, src in enumerate((p0, p1))]

    def send_halo(step, f):
        for copy in halos[step][f][0] + halos[step][f][1]:
            copy.start()
            started.append(copy)

    def arrived(first, last):
        for copy in loads[first:last]:
            copy.wait()

    arrived(2, 6)
    lane = lax.broadcasted_iota(jnp.int32, (8, LEV), 1)

    def count_body(k, total):
        at = pl.ds(pl.multiple_of(k * 32, 32), 32)
        speed = jnp.abs(wraw[0, at, :]) + jnp.abs(wraw[1, at, :])
        flag = jnp.where(speed > cfl_limit, 1.0, 0.0).astype(f32)
        return total + (flag[0:8] + flag[8:16] + flag[16:24] + flag[24:32])

    count = lax.fori_loop(0, ROWS // 32, count_body, jnp.zeros((8, LEV), f32))
    cval[0] = sum_rows(jnp.where(lane == 0, count, 0.0))
    crecv[0] = cval[0]

    def remote(src, dst, send_sem, recv_sem, peer):
        return pltpu.make_async_remote_copy(
            src_ref=src, dst_ref=dst, send_sem=send_sem, recv_sem=recv_sem, device_id=peer, device_id_type=MESH
        )

    to_root = [
        remote(
            cval.at[0],
            crecv.at[(4 - j) % 4 * Z_CHIPS + away],
            cs_sem.at[j],
            cr_sem.at[0],
            (lax.rem(y + j, 4) * Z_CHIPS + ROOT, grp),
        )
        for j in range(4)
    ]

    arrived(0, 2)
    pack(0)
    pl.semaphore_wait(barrier, jnp.where(is_root, 10, 11))
    pl.semaphore_signal(word_sem, inc=1, device_id=near[1], device_id_type=MESH)

    @pl.when(z != ROOT)
    def _():
        to_root[0].start()

    for copy in to_root[1:]:
        copy.start()
    started.extend(to_root[1:])
    send_halo(0, 0)
    arrived(6, 8)
    pack(1)
    send_halo(0, 1)

    local_step(p0, wraw, base, 0)

    arrived(8, 13)
    s_, e_, f_ = islot[...], iedge[...], iflip[...]
    is_prev, is_own = s_ < ELEMS, jnp.logical_and(s_ >= ELEMS, s_ < 2 * ELEMS)
    facing = []
    for i in range(4):
        place = jnp.full(e_.shape, EDGE_PLACE[0][i], jnp.int32)
        for s in range(1, 4):
            place = jnp.where(e_ == s, EDGE_PLACE[s][i], place)
        facing.append(place)
    tq[...] = jnp.zeros_like(tq)
    for i in range(4):
        row = (s_ & (ELEMS - 1)) + ELEMS * jnp.where(f_ == 1, facing[3 - i], facing[i])
        late = row >= PARTS[1][0]
        from_prev = row + jnp.where(late, 256, 0)
        from_next = row + jnp.where(late, 384, 256)
        target = jnp.where(is_prev, from_prev, jnp.where(is_own, row + 2 * EDGE_ROWS, from_next))
        low = target & (LEV - 1)
        tq[4 * i : 4 * i + 4, 0:ELEMS] = (target - low).astype(f32)
        tq[16 + 4 * i : 20 + 4 * i, 0:ELEMS] = low.astype(f32)
    wide = (32, 16 * LEV)
    pick = (lax.broadcasted_iota(jnp.int32, wide, 0) & 15) == (lax.broadcasted_iota(jnp.int32, wide, 1) >> 7)
    pick = jnp.where(pick, 1.0, 0.0).astype(bf16)
    bt[...] = lax.dot_general(
        tq[...].astype(bf16), pick, (((0,), (0,)), ((), ())), preferred_element_type=f32
    )[0:ELEMS]

    lanes32 = lax.broadcasted_iota(jnp.int32, (ELEMS, LEV), 1).astype(f32)

    def jm_body(k, carry):
        cell = lanes32 + (k * LEV).astype(f32)
        at = pl.ds(pl.multiple_of(k * LEV, LEV), LEV)
        for place in range(12):
            hit = None
            for s, i in SIDES[ORDER[place]]:
                col = (4 * i + s) * LEV
                one = jnp.where(bt[:, col : col + LEV] == cell, 1.0, 0.0)
                hit = one if hit is None else hit + one
            jm[place * ELEMS : (place + 1) * ELEMS, at] = hit.astype(bf16)
        return carry

    lax.fori_loop(0, 9, jm_body, 0)

    edge_scale = np.float32(time_step * penalty)

    def add_own(src, f):
        split_rows(src.at[f], rhs_own, EDGE_ROWS)
        got = jnp.dot(jm[:, 2 * EDGE_ROWS :], rhs_own[...], preferred_element_type=f32)
        base[f, 0:EDGE_ROWS, :] = base[f, 0:EDGE_ROWS, :] + edge_scale * (got[:, :LEV] + got[:, LEV:])

    def add_halo(step, f, dst):
        total = base
        for part, (first, rows) in enumerate(PARTS):
            for copy in halos[step][f][part]:
                copy.wait_recv()
            split_rows(recv.at[step, f], rhs, 2 * rows, 2 * first)
            at = slice(2 * first, 2 * (first + rows))
            got = jnp.dot(jm[:, at], rhs[at, :], preferred_element_type=f32)
            dst[f, 0:EDGE_ROWS, :] = total[f, 0:EDGE_ROWS, :] + edge_scale * (got[:, :LEV] + got[:, LEV:])
            total = dst

    add_own(p0, 0)
    local_step(p0, wraw, base, 1)
    add_own(p0, 1)

    row32 = lax.broadcasted_iota(jnp.int32, (8, LEV), 0)
    mine = (lane >> 4) == row32
    for j, ref in enumerate((iwet, idest)):
        for q in range(4):
            line = jnp.broadcast_to(ref[q : q + 1, :].astype(f32), (8, LEV))
            tq[8 * q : 8 * q + 8, :] = jnp.where(mine, line, 0.0)
        tall = (LEV, 16 * LEV)
        spread = (lax.broadcasted_iota(jnp.int32, tall, 0) & 15) == (lax.broadcasted_iota(jnp.int32, tall, 1) >> 7)
        spread = jnp.where(spread, 1.0, 0.0).astype(bf16)
        cols[j] = jnp.dot(tq[...].astype(bf16), spread, preferred_element_type=f32)

    for f in range(2):
        add_halo(0, f, p1)
        send_halo(1, f)
        p1[f, EDGE_ROWS:, :] = base[f, EDGE_ROWS:, :]
        if f == 0:
            local_step(p1, wraw, base, 0)
            add_own(p1, 0)
    local_step(p1, wraw, base, 1)
    add_own(p1, 1)

    stores = []

    def store(src, dst):
        copy = pltpu.make_async_copy(src, dst, out_sem.at[len(stores)])
        copy.start()
        stores.append(copy)

    def to_elements(src, dst, f, k):
        for n in range(16):
            at = pl.ds(pl.multiple_of(PLACE[n] * ELEMS + k * 8, 8), 8)
            dst[f, pl.ds(k * 128 + n, 8, stride=16), :] = src[f, at, :]

    def out_field(f):
        def body(k, carry):
            to_elements(base, obuf, f, k)
            return carry

        lax.fori_loop(0, ELEMS // 8, body, 0)
        store(obuf.at[f], dyn.at[f])

    add_halo(1, 0, base)
    out_field(0)

    def threshold(k, carry):
        at = pl.ds(pl.multiple_of(k * 32, 32), 32)
        condf[at, :] = jnp.exp(0.3 * base[0, at, :])
        return carry

    lax.fori_loop(0, ROWS // 32, threshold, 0)

    deep = (2 * LEV, LEV)
    above = (lax.broadcasted_iota(jnp.int32, deep, 0) & (LEV - 1)) > lax.broadcasted_iota(jnp.int32, deep, 1)
    above = jnp.where(above, 1.0, 0.0).astype(bf16)

    def columns(places, sums):
        for place in places:
            at = slice(place * ELEMS, (place + 1) * ELEMS)
            active = cols[0, :, place_lanes(place)]
            x = 2.0 * base[1, at, :] - condf[at, :]
            soft = jnp.maximum(x, 0.0) + jnp.log1p(jnp.exp(-jnp.abs(x)))
            condense = jnp.where(lanes32 < active, 0.5 * soft, 0.0)
            high = condense.astype(bf16)
            condf[at, :] = condense
            cond[at, 0:LEV] = high
            cond[at, LEV:] = (condense - high.astype(f32)).astype(bf16)
        low = places[0] * ELEMS
        flux = jnp.dot(cond[low : low + len(places) * ELEMS, :], above, preferred_element_type=f32)
        for i, place in enumerate(places):
            at = slice(place * ELEMS, (place + 1) * ELEMS)
            active = cols[0, :, place_lanes(place)]
            owner = cols[1, :, place_lanes(place)]
            evaporate = jnp.where(lanes32 < active, evap_rate * flux[i * ELEMS : (i + 1) * ELEMS, :], 0.0)
            net = condf[at, :] - evaporate
            condf[at, :] = net
            for g in range(8):
                share = jnp.where(owner == float(g), net, 0.0)
                sums[g] = sums[g] + (share[0:8] + share[8:16] + share[16:24] + share[24:32])
        return sums

    sums = columns(range(12, 16), [jnp.zeros((8, LEV), f32) for _ in range(8)])
    add_halo(1, 1, base)
    sums = columns(range(12), sums)
    for g in range(8):
        part[g] = sum_rows(sums[g])
    pl.semaphore_wait(word_sem, 1)
    rain_copies = []
    for k in (3, 2, 4, 1, 5, 0, 6):
        peer = grp_peers[k][1]
        copy = pltpu.make_async_remote_copy(
            src_ref=part.at[peer],
            dst_ref=precv.at[k],
            send_sem=rs_sem.at[k],
            recv_sem=rr_sem.at[k],
            device_id=(me, peer),
            device_id_type=MESH,
        )
        copy.start()
        rain_copies.append(copy)
        started.append(copy)
    out_field(1)

    def tend_body(k, carry):
        for n in range(16):
            at = pl.ds(pl.multiple_of(PLACE[n] * ELEMS + k * 8, 8), 8)
            spot = pl.ds(k * 128 + n, 8, stride=16)
            net = condf[at, :]
            tbuf[0, spot, :] = latent * net
            tbuf[1, spot, :] = -net
        return carry

    lax.fori_loop(0, ELEMS // 8, tend_body, 0)
    store(tbuf, tend)

    for copy in rain_copies:
        copy.wait_recv()
    collected = part[grp] + jnp.sum(precv[...], axis=0)
    lines[0] = collected * np.float32(1.0 / ROWS)

    over_grp = [remote(cval.at[1], gsum.at[k], gs_sem.at[k], gr_sem.at[k], peer) for k, peer in enumerate(grp_peers)]
    back = [remote(cval.at[2], ctot.at[0], gs_sem.at[6 + k], cr_sem.at[1], peer) for k, peer in enumerate(z_line, 1)]
    back = back[-ROOT:] + back[:-ROOT]

    @pl.when(is_root)
    def _():
        rest = crecv.at[pl.ds(1, 4 * Z_CHIPS - 1)]
        remote(rest, rest, cs_sem.at[0], cr_sem.at[0], (nxt, grp)).wait_recv()
        total = jnp.sum(crecv[...], axis=0)
        cval[1] = total
        for copy in over_grp:
            copy.start()
        for copy in over_grp:
            copy.wait_recv()
        total = total + jnp.sum(gsum[...], axis=0)
        cval[2] = total
        for copy in back:
            copy.start()
        ctot[0] = total
        for copy in over_grp + back:
            copy.wait_send()

    @pl.when(z != ROOT)
    def _():
        back[0].wait_recv()
        to_root[0].wait_send()

    lines[1] = ctot[0]
    store(lines, sums_out)
    for copy in started:
        copy.wait_send()
    for copy in stores:
        copy.wait()


def place_lanes(place):
    n = ORDER[place]
    return slice(n * LEV, (n + 1) * LEV)


def hand_over(dyn, tend, sums, dyn_out, tend_out, rain_out, cfl_out, lines, sem):
    small = pltpu.make_async_copy(sums, lines, sem.at[8])
    small.start()
    copies = []
    for src, dst in ((dyn, dyn_out), (tend, tend_out)):
        for f in range(2):
            for k in range(2):
                at = pl.ds(k * 256, 256)
                copies.append(pltpu.make_async_copy(src.at[f, at], dst.at[f, at], sem.at[len(copies)]))
                copies[-1].start()
    small.wait()
    rain_out[0] = jnp.sum(lines[0])
    cfl_out[0] = jnp.sum(lines[1])
    for copy in copies:
        copy.wait()


def shards(prognostic, wind_field, nbr_slot, nbr_edge, flip_edge, span_dest, wet_layers_present):
    f32 = jnp.float32
    anywhere = pl.BlockSpec(memory_space=pl.ANY)
    scalar = pl.BlockSpec(memory_space=pltpu.SMEM)
    vmem = pltpu.VMEM
    dma = pltpu.SemaphoreType.DMA
    whole = (2, ROWS, LEV)
    fields, tendency, sums = pl.pallas_call(
        kernel,
        out_shape=(
            jax.ShapeDtypeStruct(whole, f32),
            jax.ShapeDtypeStruct(whole, f32),
            jax.ShapeDtypeStruct((2, 1, LEV), f32),
        ),
        in_specs=[pl.BlockSpec(memory_space=pltpu.HBM)] * 7,
        out_specs=(anywhere, anywhere, anywhere),
        scratch_shapes=[
            vmem(whole, f32),
            vmem(whole, f32),
            vmem((4, ELEMS), jnp.int32),
            vmem((4, ELEMS), jnp.int32),
            vmem((4, ELEMS), jnp.int32),
            vmem((4, LEV), jnp.int32),
            vmem((4, LEV), jnp.int32),
            vmem(whole, f32),
            vmem(whole, f32),
            vmem(whole, f32),
            vmem((2, 2, 2 * EDGE_ROWS, LEV), f32),
            vmem((EDGE_ROWS, 3 * EDGE_ROWS), jnp.bfloat16),
            vmem((2 * EDGE_ROWS, 2 * LEV), jnp.bfloat16),
            vmem((EDGE_ROWS, 2 * LEV), jnp.bfloat16),
            vmem((ELEMS, LEV), f32),
            vmem((ELEMS, 16 * LEV), f32),
            vmem((2, ELEMS, 16 * LEV), f32),
            vmem((ROWS, 2 * LEV), jnp.bfloat16),
            vmem((ROWS, LEV), f32),
            vmem(whole, f32),
            vmem(whole, f32),
            vmem((3, 1, LEV), f32),
            vmem((4 * Z_CHIPS, 1, LEV), f32),
            vmem((7, 1, LEV), f32),
            vmem((1, 1, LEV), f32),
            vmem((8, 1, LEV), f32),
            vmem((7, 1, LEV), f32),
            vmem((2, 1, LEV), f32),
            dma((13,)),
            dma((2, 2, 4)),
            dma((2, 2, 4)),
            dma((4,)),
            dma((2,)),
            dma((38,)),
            dma((7,)),
            dma((7,)),
            dma((7,)),
            dma((4,)),
            pltpu.SemaphoreType.REGULAR,
        ],
        compiler_params=pltpu.CompilerParams(
            collective_id=0, has_side_effects=True, vmem_limit_bytes=52 * 1024 * 1024 + 655360
        ),
        cost_estimate=pl.CostEstimate(flops=2_000_000_000, bytes_accessed=2_200_000, transcendentals=200_000),
        name="steps_and_columns",
    )(
        prognostic.reshape(whole),
        wind_field.reshape(whole),
        nbr_slot.T,
        nbr_edge.T,
        flip_edge.T,
        span_dest.reshape(4, LEV),
        wet_layers_present.reshape(4, LEV),
    )
    fields, tendency, rain, cfl = pl.pallas_call(
        hand_over,
        out_shape=(
            jax.ShapeDtypeStruct(whole, f32),
            jax.ShapeDtypeStruct(whole, f32),
            jax.ShapeDtypeStruct((1,), f32),
            jax.ShapeDtypeStruct((1,), f32),
        ),
        in_specs=[anywhere, anywhere, anywhere],
        out_specs=(anywhere, anywhere, scalar, scalar),
        scratch_shapes=[vmem((2, 1, LEV), f32), dma((9,))],
        compiler_params=pltpu.CompilerParams(vmem_limit_bytes=6 * 1024 * 1024),
        name="hand_over",
    )(fields, tendency, sums)
    shape = prognostic.shape
    return fields.reshape(shape), tendency.reshape(shape), rain, cfl.reshape(())


def solution(mesh):
    in_specs = (
        P(None, ("elem", "grp"), None, None),
        P(None, ("elem", "grp"), None, None),
        P(("elem", "grp"), None),
        P(("elem", "grp"), None),
        P(("elem", "grp"), None),
        P(("elem", "grp"), None),
        P(("elem", "grp")),
    )
    out_specs = (
        P(None, ("elem", "grp"), None, None),
        P(None, ("elem", "grp"), None, None),
        P(("elem", "grp")),
        P(),
    )
    return jax.shard_map(shards, mesh=mesh, in_specs=in_specs, out_specs=out_specs, check_vma=False)
```

```python
import math

import jax
import jax.numpy as jnp
import numpy as np
from jax import lax
from jax.experimental import pallas as pl
from jax.experimental.pallas import tpu as pltpu
from jax.sharding import PartitionSpec as P

STEPS = 2
ELEMS = 32
ROWS = 512
LEV = 128
EDGE_ROWS = 384
PARTS = ((0, EDGE_ROWS),)

edge_nodes = np.array([[0, 1, 2, 3], [3, 7, 11, 15], [12, 13, 14, 15], [0, 4, 8, 12]])
time_step = 0.02
viscosity = 0.05
penalty = 4.0
cfl_limit = 2.0
latent = 1.5
evap_rate = 0.02

ORDER = [0, 1, 2, 3, 4, 7, 8, 11, 12, 13, 14, 15, 5, 6, 9, 10]
PLACE = {n: p for p, n in enumerate(ORDER)}
EDGE_PLACE = [[PLACE[int(n)] for n in nodes] for nodes in edge_nodes]
SIDES = {n: [(s, i) for s in range(4) for i in range(4) if edge_nodes[s][i] == n] for n in range(16)}

Z_CHIPS = 32
ROOT = 4
MESH = pl.DeviceIdType.MESH


def nodal_derivative_matrix():
    points = np.array([-1.0, -1.0 / math.sqrt(5.0), 1.0 / math.sqrt(5.0), 1.0])
    off_diag = points[:, None] - points[None, :] + np.eye(4)
    weights = 1.0 / np.prod(off_diag, axis=1)
    derivative = weights[None, :] / weights[:, None] / off_diag
    derivative = derivative * (1.0 - np.eye(4))
    return derivative - np.eye(4) * np.sum(derivative, axis=1)[:, None]


D1 = nodal_derivative_matrix()
D2 = D1 @ D1


def weighted(coefs, values):
    total = None
    for coef, value in zip(coefs, values):
        if abs(coef) < 1e-12:
            continue
        term = value * np.float32(coef)
        total = term if total is None else total + term
    return total


def split_rows(src, dst, rows, first=0):
    step = 64

    def body(k, carry):
        at = pl.ds(pl.multiple_of(first + k * step, step), step)
        x = src[at, :]
        high = x.astype(jnp.bfloat16)
        dst[at, 0:LEV] = high
        dst[at, LEV : 2 * LEV] = (x - high.astype(jnp.float32)).astype(jnp.bfloat16)
        return carry

    lax.fori_loop(0, rows // step, body, 0)


def local_step(src, wind, base, f):
    def body(k, carry):
        at = lambda n: pl.ds(pl.multiple_of(PLACE[n] * ELEMS + k * 8, 8), 8)
        F = [src[f, at(n), :] for n in range(16)]
        for n in range(16):
            r, c = divmod(n, 4)
            row = [F[4 * r + b] for b in range(4)]
            col = [F[4 * b + c] for b in range(4)]
            u = wind[0, pl.ds(k * 128 + n, 8, stride=16), :]
            v = wind[1, pl.ds(k * 128 + n, 8, stride=16), :]
            grad_col = weighted(D1[c] * -time_step, row)
            grad_row = weighted(D1[r] * -time_step, col)
            centre = 1.0 - time_step * penalty * len(SIDES[n])
            centre = centre + time_step * viscosity * (D2[c][c] + D2[r][r])
            others = [b for b in range(4) if b != c]
            others_r = [b for b in range(4) if b != r]
            lap = weighted(
                [centre]
                + [time_step * viscosity * D2[c][b] for b in others]
                + [time_step * viscosity * D2[r][b] for b in others_r],
                [F[n]] + [row[b] for b in others] + [col[b] for b in others_r],
            )
            base[f, at(n), :] = lap + u * grad_col + v * grad_row
        return carry

    lax.fori_loop(0, ELEMS // 8, body, 0)


def sum_rows(x):
    return jnp.sum(x, axis=0, keepdims=True)


def kernel(
    prog, wind, slot, edge, flip, dest, wet,
    dyn, tend, sums_out,
    praw, wraw, islot, iedge, iflip, idest, iwet,
    p0, p1, base, recv, jm, rhs, rhs_own, tq, bt, cols, cond, condf, obuf, tbuf,
    cval, crecv, gsum, ctot, part, precv, lines,
    in_sem, hs_sem, hr_sem, cs_sem, cr_sem, gs_sem, gr_sem, rs_sem, rr_sem, out_sem, word_sem,
):
    f32, bf16 = jnp.float32, jnp.bfloat16
    me = lax.axis_index("elem")
    grp = lax.axis_index("grp")
    n_elem = lax.axis_size("elem")
    nxt, prv = lax.rem(me + 1, n_elem), lax.rem(me + n_elem - 1, n_elem)
    y, z = me // Z_CHIPS, lax.rem(me, Z_CHIPS)
    grp_peers = [(me, lax.rem(grp + k, 8)) for k in range(1, 8)]
    z_line = [(y * Z_CHIPS + lax.rem(ROOT + k, Z_CHIPS), grp) for k in range(1, Z_CHIPS)]
    away = lax.rem(z + Z_CHIPS - ROOT, Z_CHIPS)
    is_root = z == ROOT

    halves = lambda src, dst: [(src.at[pl.ds(k, 256)], dst.at[pl.ds(k, 256)]) for k in (0, 256)]
    pieces = halves(prog.at[0], praw.at[0])
    pieces += halves(wind.at[0], wraw.at[0]) + halves(wind.at[1], wraw.at[1])
    pieces += halves(prog.at[1], praw.at[1])
    pieces += [(slot, islot), (edge, iedge), (flip, iflip), (dest, idest), (wet, iwet)]
    loads = [pltpu.make_async_copy(src, dst, in_sem.at[i]) for i, (src, dst) in enumerate(pieces)]
    for copy in loads:
        copy.start()

    barrier = pltpu.get_barrier_semaphore()

    def greet(peer):
        pl.semaphore_signal(barrier, inc=1, device_id=peer, device_id_type=MESH)

    near = [(me, lax.rem(grp + 2 * i, 8)) for i in (1, 3)]
    core = lax.rem(grp, 2)
    near += [(me, lax.rem(grp - core + 2 * i, 8) + 1 - core) for i in (0, 1, 3)]
    for peer in [(nxt, grp), (prv, grp)] + near:
        greet(peer)

    @pl.when(is_root)
    def _():
        def greet_body(k, carry):
            greet((lax.rem(y + k // Z_CHIPS, 4) * Z_CHIPS + lax.rem(ROOT + lax.rem(k, Z_CHIPS), Z_CHIPS), grp))
            return carry

        lax.fori_loop(1, 4 * Z_CHIPS, greet_body, 0)

    def pack(f):
        def body(k, carry):
            for n in range(16):
                at = pl.ds(pl.multiple_of(PLACE[n] * ELEMS + k * 8, 8), 8)
                p0[f, at, :] = praw[f, pl.ds(k * 128 + n, 8, stride=16), :]
            return carry

        lax.fori_loop(0, ELEMS // 8, body, 0)

    def halo(step, src, f, part):
        first, rows = PARTS[part]
        return [
            pltpu.make_async_remote_copy(
                src_ref=src.at[f, pl.ds(first, rows)],
                dst_ref=recv.at[step, f, pl.ds(2 * first + way * rows, rows)],
                send_sem=hs_sem.at[step, f, 2 * part + way],
                recv_sem=hr_sem.at[step, f, 2 * part + way],
                device_id=(target, grp),
                device_id_type=MESH,
            )
            for way, target in enumerate((nxt, prv))
        ]

    started = []
    halos = [[[halo(s, src, f, p) for p in range(len(PARTS))] for f in range(2)] for s, src in enumerate((p0, p1))]

    def send_halo(step, f):
        for copy in sum(halos[step][f], []):
            copy.start()
            started.append(copy)

    def arrived(first, last):
        for copy in loads[first:last]:
            copy.wait()

    arrived(2, 6)
    lane = lax.broadcasted_iota(jnp.int32, (8, LEV), 1)

    def count_body(k, total):
        at = pl.ds(pl.multiple_of(k * 32, 32), 32)
        speed = jnp.abs(wraw[0, at, :]) + jnp.abs(wraw[1, at, :])
        flag = jnp.where(speed > cfl_limit, 1.0, 0.0).astype(f32)
        return total + (flag[0:8] + flag[8:16] + flag[16:24] + flag[24:32])

    count = lax.fori_loop(0, ROWS // 32, count_body, jnp.zeros((8, LEV), f32))
    cval[0] = sum_rows(jnp.where(lane == 0, count, 0.0))
    crecv[0] = cval[0]

    def remote(src, dst, send_sem, recv_sem, peer):
        return pltpu.make_async_remote_copy(
            src_ref=src, dst_ref=dst, send_sem=send_sem, recv_sem=recv_sem, device_id=peer, device_id_type=MESH
        )

    to_root = [
        remote(
            cval.at[0],
            crecv.at[(4 - j) % 4 * Z_CHIPS + away],
            cs_sem.at[j],
            cr_sem.at[0],
            (lax.rem(y + j, 4) * Z_CHIPS + ROOT, grp),
        )
        for j in range(4)
    ]

    arrived(0, 2)
    pack(0)
    pl.semaphore_wait(barrier, jnp.where(is_root, 10, 11))
    pl.semaphore_signal(word_sem, inc=1, device_id=near[1], device_id_type=MESH)

    @pl.when(z != ROOT)
    def _():
        to_root[0].start()

    for copy in to_root[1:]:
        copy.start()
    started.extend(to_root[1:])
    send_halo(0, 0)
    arrived(6, 8)
    pack(1)
    send_halo(0, 1)

    local_step(p0, wraw, base, 0)

    arrived(8, 13)
    s_, e_, f_ = islot[...], iedge[...], iflip[...]
    is_prev, is_own = s_ < ELEMS, jnp.logical_and(s_ >= ELEMS, s_ < 2 * ELEMS)
    facing = []
    for i in range(4):
        place = jnp.full(e_.shape, EDGE_PLACE[0][i], jnp.int32)
        for s in range(1, 4):
            place = jnp.where(e_ == s, EDGE_PLACE[s][i], place)
        facing.append(place)
    tq[...] = jnp.zeros_like(tq)
    for i in range(4):
        row = (s_ & (ELEMS - 1)) + ELEMS * jnp.where(f_ == 1, facing[3 - i], facing[i])
        target = row + jnp.where(is_prev, 0, jnp.where(is_own, 2 * EDGE_ROWS, EDGE_ROWS))
        low = target & (LEV - 1)
        tq[4 * i : 4 * i + 4, 0:ELEMS] = (target - low).astype(f32)
        tq[16 + 4 * i : 20 + 4 * i, 0:ELEMS] = low.astype(f32)
    wide = (32, 16 * LEV)
    pick = (lax.broadcasted_iota(jnp.int32, wide, 0) & 15) == (lax.broadcasted_iota(jnp.int32, wide, 1) >> 7)
    pick = jnp.where(pick, 1.0, 0.0).astype(bf16)
    bt[...] = lax.dot_general(
        tq[...].astype(bf16), pick, (((0,), (0,)), ((), ())), preferred_element_type=f32
    )[0:ELEMS]

    lanes32 = lax.broadcasted_iota(jnp.int32, (ELEMS, LEV), 1).astype(f32)

    def jm_body(k, carry):
        cell = lanes32 + (k * LEV).astype(f32)
        at = pl.ds(pl.multiple_of(k * LEV, LEV), LEV)
        for place in range(12):
            hit = None
            for s, i in SIDES[ORDER[place]]:
                col = (4 * i + s) * LEV
                one = jnp.where(bt[:, col : col + LEV] == cell, 1.0, 0.0)
                hit = one if hit is None else hit + one
            jm[place * ELEMS : (place + 1) * ELEMS, at] = hit.astype(bf16)
        return carry

    lax.fori_loop(0, 9, jm_body, 0)

    edge_scale = np.float32(time_step * penalty)

    def add_own(src, f):
        split_rows(src.at[f], rhs_own, EDGE_ROWS)
        got = jnp.dot(jm[:, 2 * EDGE_ROWS :], rhs_own[...], preferred_element_type=f32)
        base[f, 0:EDGE_ROWS, :] = base[f, 0:EDGE_ROWS, :] + edge_scale * (got[:, :LEV] + got[:, LEV:])

    def add_halo(step, f, dst):
        total = base
        for part, (first, rows) in enumerate(PARTS):
            for copy in halos[step][f][part]:
                copy.wait_recv()
            split_rows(recv.at[step, f], rhs, 2 * rows, 2 * first)
            at = slice(2 * first, 2 * (first + rows))
            got = jnp.dot(jm[:, at], rhs[at, :], preferred_element_type=f32)
            dst[f, 0:EDGE_ROWS, :] = total[f, 0:EDGE_ROWS, :] + edge_scale * (got[:, :LEV] + got[:, LEV:])
            total = dst

    add_own(p0, 0)
    local_step(p0, wraw, base, 1)
    add_own(p0, 1)

    row32 = lax.broadcasted_iota(jnp.int32, (8, LEV), 0)
    mine = (lane >> 4) == row32
    for j, ref in enumerate((iwet, idest)):
        for q in range(4):
            line = jnp.broadcast_to(ref[q : q + 1, :].astype(f32), (8, LEV))
            tq[8 * q : 8 * q + 8, :] = jnp.where(mine, line, 0.0)
        tall = (LEV, 16 * LEV)
        spread = (lax.broadcasted_iota(jnp.int32, tall, 0) & 15) == (lax.broadcasted_iota(jnp.int32, tall, 1) >> 7)
        spread = jnp.where(spread, 1.0, 0.0).astype(bf16)
        cols[j] = jnp.dot(tq[...].astype(bf16), spread, preferred_element_type=f32)

    for f in range(2):
        add_halo(0, f, p1)
        send_halo(1, f)
        p1[f, EDGE_ROWS:, :] = base[f, EDGE_ROWS:, :]
        if f == 0:
            local_step(p1, wraw, base, 0)
            add_own(p1, 0)
    local_step(p1, wraw, base, 1)
    add_own(p1, 1)

    stores = []

    def store(src, dst):
        copy = pltpu.make_async_copy(src, dst, out_sem.at[len(stores)])
        copy.start()
        stores.append(copy)

    def to_elements(src, dst, f, k):
        for n in range(16):
            at = pl.ds(pl.multiple_of(PLACE[n] * ELEMS + k * 8, 8), 8)
            dst[f, pl.ds(k * 128 + n, 8, stride=16), :] = src[f, at, :]

    def out_field(f):
        def body(k, carry):
            to_elements(base, obuf, f, k)
            return carry

        lax.fori_loop(0, ELEMS // 8, body, 0)
        store(obuf.at[f], dyn.at[f])

    add_halo(1, 0, base)
    out_field(0)

    def threshold(k, carry):
        at = pl.ds(pl.multiple_of(k * 32, 32), 32)
        condf[at, :] = jnp.exp(0.3 * base[0, at, :])
        return carry

    lax.fori_loop(0, ROWS // 32, threshold, 0)

    deep = (2 * LEV, LEV)
    above = (lax.broadcasted_iota(jnp.int32, deep, 0) & (LEV - 1)) > lax.broadcasted_iota(jnp.int32, deep, 1)
    above = jnp.where(above, 1.0, 0.0).astype(bf16)

    def columns(places, sums):
        for place in places:
            at = slice(place * ELEMS, (place + 1) * ELEMS)
            active = cols[0, :, place_lanes(place)]
            x = 2.0 * base[1, at, :] - condf[at, :]
            soft = jnp.maximum(x, 0.0) + jnp.log1p(jnp.exp(-jnp.abs(x)))
            condense = jnp.where(lanes32 < active, 0.5 * soft, 0.0)
            high = condense.astype(bf16)
            condf[at, :] = condense
            cond[at, 0:LEV] = high
            cond[at, LEV:] = (condense - high.astype(f32)).astype(bf16)
        low = places[0] * ELEMS
        flux = jnp.dot(cond[low : low + len(places) * ELEMS, :], above, preferred_element_type=f32)
        for i, place in enumerate(places):
            at = slice(place * ELEMS, (place + 1) * ELEMS)
            active = cols[0, :, place_lanes(place)]
            owner = cols[1, :, place_lanes(place)]
            evaporate = jnp.where(lanes32 < active, evap_rate * flux[i * ELEMS : (i + 1) * ELEMS, :], 0.0)
            net = condf[at, :] - evaporate
            condf[at, :] = net
            for g in range(8):
                share = jnp.where(owner == float(g), net, 0.0)
                sums[g] = sums[g] + (share[0:8] + share[8:16] + share[16:24] + share[24:32])
        return sums

    sums = columns(range(12, 16), [jnp.zeros((8, LEV), f32) for _ in range(8)])
    add_halo(1, 1, base)
    sums = columns(range(12), sums)
    for g in range(8):
        part[g] = sum_rows(sums[g])
    pl.semaphore_wait(word_sem, 1)
    rain_copies = []
    for k in (3, 2, 4, 1, 5, 0, 6):
        peer = grp_peers[k][1]
        copy = pltpu.make_async_remote_copy(
            src_ref=part.at[peer],
            dst_ref=precv.at[k],
            send_sem=rs_sem.at[k],
            recv_sem=rr_sem.at[k],
            device_id=(me, peer),
            device_id_type=MESH,
        )
        copy.start()
        rain_copies.append(copy)
        started.append(copy)
    out_field(1)

    def tend_body(k, carry):
        for n in range(16):
            at = pl.ds(pl.multiple_of(PLACE[n] * ELEMS + k * 8, 8), 8)
            spot = pl.ds(k * 128 + n, 8, stride=16)
            net = condf[at, :]
            tbuf[0, spot, :] = latent * net
            tbuf[1, spot, :] = -net
        return carry

    lax.fori_loop(0, ELEMS // 8, tend_body, 0)
    store(tbuf, tend)

    for copy in rain_copies:
        copy.wait_recv()
    collected = part[grp] + jnp.sum(precv[...], axis=0)
    lines[0] = collected * np.float32(1.0 / ROWS)

    over_grp = [remote(cval.at[1], gsum.at[k], gs_sem.at[k], gr_sem.at[k], peer) for k, peer in enumerate(grp_peers)]
    back = [remote(cval.at[2], ctot.at[0], gs_sem.at[6 + k], cr_sem.at[1], peer) for k, peer in enumerate(z_line, 1)]
    back = back[-ROOT:] + back[:-ROOT]

    @pl.when(is_root)
    def _():
        rest = crecv.at[pl.ds(1, 4 * Z_CHIPS - 1)]
        remote(rest, rest, cs_sem.at[0], cr_sem.at[0], (nxt, grp)).wait_recv()
        total = jnp.sum(crecv[...], axis=0)
        cval[1] = total
        for copy in over_grp:
            copy.start()
        for copy in over_grp:
            copy.wait_recv()
        total = total + jnp.sum(gsum[...], axis=0)
        cval[2] = total
        for copy in back:
            copy.start()
        ctot[0] = total
        for copy in over_grp + back:
            copy.wait_send()

    @pl.when(z != ROOT)
    def _():
        back[0].wait_recv()
        to_root[0].wait_send()

    lines[1] = ctot[0]
    store(lines, sums_out)
    for copy in started:
        copy.wait_send()
    for copy in stores:
        copy.wait()


def place_lanes(place):
    n = ORDER[place]
    return slice(n * LEV, (n + 1) * LEV)


def hand_over(dyn, tend, sums, dyn_out, tend_out, rain_out, cfl_out, lines, sem):
    small = pltpu.make_async_copy(sums, lines, sem.at[8])
    small.start()
    copies = []
    for src, dst in ((dyn, dyn_out), (tend, tend_out)):
        for f in range(2):
            for k in range(2):
                at = pl.ds(k * 256, 256)
                copies.append(pltpu.make_async_copy(src.at[f, at], dst.at[f, at], sem.at[len(copies)]))
                copies[-1].start()
    small.wait()
    rain_out[0] = jnp.sum(lines[0])
    cfl_out[0] = jnp.sum(lines[1])
    for copy in copies:
        copy.wait()


def shards(prognostic, wind_field, nbr_slot, nbr_edge, flip_edge, span_dest, wet_layers_present):
    f32 = jnp.float32
    anywhere = pl.BlockSpec(memory_space=pl.ANY)
    scalar = pl.BlockSpec(memory_space=pltpu.SMEM)
    vmem = pltpu.VMEM
    dma = pltpu.SemaphoreType.DMA
    whole = (2, ROWS, LEV)
    fields, tendency, sums = pl.pallas_call(
        kernel,
        out_shape=(
            jax.ShapeDtypeStruct(whole, f32),
            jax.ShapeDtypeStruct(whole, f32),
            jax.ShapeDtypeStruct((2, 1, LEV), f32),
        ),
        in_specs=[pl.BlockSpec(memory_space=pltpu.HBM)] * 7,
        out_specs=(anywhere, anywhere, anywhere),
        scratch_shapes=[
            vmem(whole, f32),
            vmem(whole, f32),
            vmem((4, ELEMS), jnp.int32),
            vmem((4, ELEMS), jnp.int32),
            vmem((4, ELEMS), jnp.int32),
            vmem((4, LEV), jnp.int32),
            vmem((4, LEV), jnp.int32),
            vmem(whole, f32),
            vmem(whole, f32),
            vmem(whole, f32),
            vmem((2, 2, 2 * EDGE_ROWS, LEV), f32),
            vmem((EDGE_ROWS, 3 * EDGE_ROWS), jnp.bfloat16),
            vmem((2 * EDGE_ROWS, 2 * LEV), jnp.bfloat16),
            vmem((EDGE_ROWS, 2 * LEV), jnp.bfloat16),
            vmem((ELEMS, LEV), f32),
            vmem((ELEMS, 16 * LEV), f32),
            vmem((2, ELEMS, 16 * LEV), f32),
            vmem((ROWS, 2 * LEV), jnp.bfloat16),
            vmem((ROWS, LEV), f32),
            vmem(whole, f32),
            vmem(whole, f32),
            vmem((3, 1, LEV), f32),
            vmem((4 * Z_CHIPS, 1, LEV), f32),
            vmem((7, 1, LEV), f32),
            vmem((1, 1, LEV), f32),
            vmem((8, 1, LEV), f32),
            vmem((7, 1, LEV), f32),
            vmem((2, 1, LEV), f32),
            dma((13,)),
            dma((2, 2, 2)),
            dma((2, 2, 2)),
            dma((4,)),
            dma((2,)),
            dma((38,)),
            dma((7,)),
            dma((7,)),
            dma((7,)),
            dma((4,)),
            pltpu.SemaphoreType.REGULAR,
        ],
        compiler_params=pltpu.CompilerParams(
            collective_id=0, has_side_effects=True, vmem_limit_bytes=52 * 1024 * 1024 + 655360
        ),
        cost_estimate=pl.CostEstimate(flops=2_000_000_000, bytes_accessed=2_200_000, transcendentals=200_000),
        name="steps_and_columns",
    )(
        prognostic.reshape(whole),
        wind_field.reshape(whole),
        nbr_slot.T,
        nbr_edge.T,
        flip_edge.T,
        span_dest.reshape(4, LEV),
        wet_layers_present.reshape(4, LEV),
    )
    fields, tendency, rain, cfl = pl.pallas_call(
        hand_over,
        out_shape=(
            jax.ShapeDtypeStruct(whole, f32),
            jax.ShapeDtypeStruct(whole, f32),
            jax.ShapeDtypeStruct((1,), f32),
            jax.ShapeDtypeStruct((1,), f32),
        ),
        in_specs=[anywhere, anywhere, anywhere],
        out_specs=(anywhere, anywhere, scalar, scalar),
        scratch_shapes=[vmem((2, 1, LEV), f32), dma((9,))],
        compiler_params=pltpu.CompilerParams(vmem_limit_bytes=6 * 1024 * 1024),
        name="hand_over",
    )(fields, tendency, sums)
    shape = prognostic.shape
    return fields.reshape(shape), tendency.reshape(shape), rain, cfl.reshape(())


def solution(mesh):
    in_specs = (
        P(None, ("elem", "grp"), None, None),
        P(None, ("elem", "grp"), None, None),
        P(("elem", "grp"), None),
        P(("elem", "grp"), None),
        P(("elem", "grp"), None),
        P(("elem", "grp"), None),
        P(("elem", "grp")),
    )
    out_specs = (
        P(None, ("elem", "grp"), None, None),
        P(None, ("elem", "grp"), None, None),
        P(("elem", "grp")),
        P(),
    )
    return jax.shard_map(shards, mesh=mesh, in_specs=in_specs, out_specs=out_specs, check_vma=False)
```
